128 devices in a mesh: node: 8 (over x, y_lo), local: 16 (over z, y_hi, core).
Axes of the slice: x: 4, y: 4 (y_hi: 2, y_lo: 2; y = y_hi * 2 + y_lo), z: 4, core: 2. Of those that a mesh axis runs over, the one named last changes fastest.
Arguments:
- inputs: bfloat16 [4096, 4096], P(('node', 'local')), may hold values from -24 to 24
- hidden_grad: bfloat16 [4096, 16384], P('node', 'local'), may hold values from -1.5 to 1.5
- w_gate: bfloat16 [4096, 16384], P('node', 'local'), may hold values from -0.09375 to 0.09375
- w_up: bfloat16 [4096, 16384], P('node', 'local'), may hold values from -0.09375 to 0.09375
Outputs:
- input_grad: bfloat16 [4096, 4096], P(('node', 'local'))
- gate_grad: float32 [4096, 16384], P('node', 'local')
- up_grad: float32 [4096, 16384], P('node', 'local')
The draws below stay inside these ranges and needn't reach their ends.
All inputs are finite; a program needn't handle non-finite values.
Results may differ from the reference program's by a relative error of at most 0.019.
Values may be sent and summed in bfloat16 or wider, within the bound.
No kernel may reach another device: no remote copies, remote signals or barrier semaphores. Data moves between devices by JAX's collectives and lax.ppermute only.
A program may use at most 128 MiB of HBM per device.

```python
import jax
import jax.numpy as jnp
from jax import lax

D = 4096
FF = 16384
NODE_TOK = 512
TOKENS = 4096
N_NODE = 8


def strengthened(values, rng, source, target, parts, factor):
    def block_of(dim):
        return (jnp.arange(values.shape[dim]) // (values.shape[dim] // parts)).reshape((-1,) + (1,) * (values.ndim - 1 - dim))

    one_side = jax.random.permutation(rng, parts)[block_of(target)]
    far = (block_of(target) + parts // 2) % parts
    return jnp.where((block_of(source) == one_side) | (block_of(source) == far), factor * values, values)


def shard_levels(key, shape, split, least, largest):
    loudness = 1.0
    for axis_at, shards_of in split:
        steps = jax.random.uniform(jax.random.fold_in(jax.random.fold_in(key, 6), axis_at), (shards_of,), jnp.float32, least / len(split), largest / len(split))
        loudness = loudness * jnp.repeat(jnp.exp(steps), shape[axis_at] // shards_of).reshape((-1,) + (1,) * (len(shape) - 1 - axis_at))
    return loudness


def scatter_about(rng, shape, spread, bound, pieces=(), held_as=jnp.bfloat16):
    drawn = jax.random.normal(rng, shape, jnp.float32) * spread
    if len(pieces) > 0:
        drawn = shard_levels(rng, shape, pieces, -0.22, 0.18) * drawn
    return jnp.clip(drawn, min=-bound, max=bound).astype(held_as)


def noise_with(own_key, shape, width, reach, pieces, heavy, kind=jnp.bfloat16):
    array = width * jax.random.normal(own_key, shape, jnp.float32)
    if pieces:
        array = array * shard_levels(own_key, shape, pieces, -0.22, 0.18)
    return jnp.clip(strengthened(array, jax.random.fold_in(own_key, 3), *heavy), -reach, reach).astype(kind)


def setup_inputs(seed: int = 0) -> dict:
    keys = jax.random.split(jax.random.key(seed), 5)
    return {
        "inputs": noise_with(keys[0], (TOKENS, D), 1.0, 24.0, ((0, 128),), (0, 1, 128, 5.5)),
        "hidden_grad": noise_with(keys[1], (TOKENS, FF), 0.25, 1.5, ((0, 8), (1, 16)), (1, 0, 16, 2.0)),
        "w_gate": scatter_about(keys[2], (D, FF), D ** -0.5, 0.09375, ((0, 8), (1, 16))),
        "w_up": scatter_about(keys[3], (D, FF), D ** -0.5, 0.09375, ((0, 8), (1, 16))),
    }


def reference(inputs, hidden_grad, w_gate, w_up):
    gate = jnp.dot(inputs, w_gate, preferred_element_type=jnp.float32)
    upper = jnp.dot(inputs, w_up, preferred_element_type=jnp.float32)
    sigma = jax.nn.sigmoid(gate)
    grad_f = hidden_grad.astype(jnp.float32)
    up_delta = (grad_f * gate * sigma).astype(jnp.bfloat16)
    gate_delta = (grad_f * upper * sigma * (1.0 + gate * (1.0 - sigma))).astype(jnp.bfloat16)
    input_grad = (jnp.dot(gate_delta, w_gate.T, preferred_element_type=jnp.float32)
                  + jnp.dot(up_delta, w_up.T, preferred_element_type=jnp.float32)).astype(jnp.bfloat16)
    group = NODE_TOK
    gate_grad = jnp.zeros((D, FF), jnp.float32)
    up_grad = jnp.zeros((D, FF), jnp.float32)
    for member in range(N_NODE):
        rows = inputs[member * group:(member + 1) * group]
        part_gate = jnp.dot(rows.T, gate_delta[member * group:(member + 1) * group], preferred_element_type=jnp.float32).astype(jnp.bfloat16)
        part_up = jnp.dot(rows.T, up_delta[member * group:(member + 1) * group], preferred_element_type=jnp.float32).astype(jnp.bfloat16)
        part_gate, part_up = lax.optimization_barrier((part_gate, part_up))
        gate_grad = gate_grad + part_gate.astype(jnp.float32)
        up_grad = up_grad + part_up.astype(jnp.float32)
    return input_grad, gate_grad, up_grad
```

```python
import jax
import jax.numpy as jnp
from jax import lax
from jax.sharding import PartitionSpec as P

AXES = ("node", "local")
CHUNKS = 2


def place(i):
    n, l = divmod(i, 16)
    return (n // 2, n % 2, l // 4, (l // 2) % 2, l % 2)


def index(x, yl, z, yh, c):
    return (x * 2 + yl) * 16 + z * 4 + yh * 2 + c


def pairs(move):
    return [(i, index(*move(*place(i)))) for i in range(128)]


XUP = pairs(lambda x, yl, z, yh, c: ((x + 1) % 4, yl, z, yh, c))
XDOWN = pairs(lambda x, yl, z, yh, c: ((x + 3) % 4, yl, z, yh, c))
YLO = pairs(lambda x, yl, z, yh, c: (x, 1 - yl, z, yh, c))
YBOTH = pairs(lambda x, yl, z, yh, c: (x, 1 - yl, z, 1 - yh, c))
ZLO = pairs(lambda x, yl, z, yh, c: (x, yl, z ^ 1, yh, c))
ZBOTH = pairs(lambda x, yl, z, yh, c: (x, yl, 3 - z, yh, c))
CORE = pairs(lambda x, yl, z, yh, c: (x, yl, z, yh, 1 - c))


def send(value, to):
    return lax.ppermute(value, AXES, to)


def pick(value, at, axis):
    return lax.dynamic_index_in_dim(value, at, axis, keepdims=False)


def join(own, other, bit):
    where = lax.broadcasted_iota(jnp.int32, (2,) + own.shape, 0) == bit
    return jnp.where(where, own[None], other[None])


def gather(value, steps):
    for to, bit in steps:
        value = join(value, send(value, to), bit)
    return value


def scatter_sum(value, steps):
    for to, bit, axis in steps:
        other = send(pick(value, 1 - bit, axis), to)
        value = (
            pick(value, bit, axis).astype(jnp.float32) + other.astype(jnp.float32)
        ).astype(jnp.bfloat16)
    return value


def dot(a, b, ca, cb):
    return lax.dot_general(a, b, (((ca,), (cb,)), ((), ())), preferred_element_type=jnp.float32)


def shards(inputs, hidden_grad, w_gate, w_up):
    node, local = lax.axis_index("node"), lax.axis_index("local")
    x, yl = node // 2, node % 2
    zh, zl, yh, c = local // 8, (local // 4) % 2, (local // 2) % 2, local % 2
    bf = jnp.bfloat16

    width = 512 // CHUNKS
    both = jnp.stack(
        [w_gate.reshape(512, 2, CHUNKS, width), w_up.reshape(512, 2, CHUNKS, width)], 3
    )
    mine, theirs = pick(both, yl, 1), pick(both, 1 - yl, 1)

    weights = []
    for k in range(CHUNKS):
        own = mine[:, k].reshape(512, 2 * width)
        other = send(theirs[:, k].reshape(512, 2 * width), YLO)
        block = join(own, other, yl).reshape(1024, 2 * width)
        from_down, from_up = send(block, XUP), send(block, XDOWN)
        far_a, far_b = send(from_down[:512], XUP), send(from_up[512:], XDOWN)
        weights.append([[block], [from_up], [far_a, far_b], [from_down]])

    rolled = jnp.take(inputs.reshape(32, 4, 1024), (x + jnp.arange(4)) % 4, axis=1)
    first = gather(
        rolled[:, :2].reshape(32, 2048), [(YLO, yl), (YBOTH, yh), (ZLO, zl), (ZBOTH, zh), (CORE, c)]
    )
    second = gather(
        rolled[:, 2:].reshape(32, 2048), [(ZLO, zl), (ZBOTH, zh), (YLO, yl), (YBOTH, yh), (CORE, c)]
    )
    first = first.reshape(1024, 2048)
    second = second.transpose(0, 3, 4, 1, 2, 5, 6).reshape(1024, 2048)
    tokens = [first[:, :1024], first[:, 1024:], second[:, :1024], second[:, 1024:]]

    hidden = hidden_grad.reshape(512, 2, 512)
    hidden = join(pick(hidden, yl, 1), send(pick(hidden, 1 - yl, 1), YLO), yl)
    hidden = (
        hidden.reshape(2, 2, 2, 2, 2, 32, 512).transpose(4, 1, 2, 3, 0, 5, 6).reshape(1024, 512)
    )

    deltas, parts = [], []
    for k in range(CHUNKS):
        total = None
        for d in (0, 1, 3, 2):
            pieces = weights[k][d]
            rows = 1024 // len(pieces)
            for j, piece in enumerate(pieces):
                term = dot(tokens[d][:, j * rows : (j + 1) * rows], piece, 1, 0)
                total = term if total is None else total + term
        gate, upper = total[:, :width], total[:, width:]
        sigma = jax.nn.sigmoid(gate)
        grad_f = hidden[:, k * width : (k + 1) * width].astype(jnp.float32)
        up_delta = (grad_f * gate * sigma).astype(bf)
        gate_delta = (grad_f * upper * sigma * (1.0 + gate * (1.0 - sigma))).astype(bf)
        delta = jnp.concatenate([gate_delta, up_delta], axis=1)
        deltas.append(delta)

        far = dot(tokens[2], delta, 0, 0).astype(bf)
        up, down = dot(tokens[1], delta, 0, 0), dot(tokens[3], delta, 0, 0)
        a, b = send(far[:512], XUP), send(far[512:], XDOWN)
        up = jnp.concatenate([up[:512] + a.astype(jnp.float32), up[512:]], 0).astype(bf)
        down = jnp.concatenate([down[:512], down[512:] + b.astype(jnp.float32)], 0).astype(bf)
        a, b = send(up, XUP), send(down, XDOWN)
        total = dot(tokens[0], delta, 0, 0) + a.astype(jnp.float32) + b.astype(jnp.float32)
        total = total.reshape(2, 512, 2 * width)
        other = send(pick(total, 1 - yl, 0).astype(bf), YLO)
        parts.append(
            join(pick(total, yl, 0), other.astype(jnp.float32), yl).reshape(2, 512, 2, width)
        )

    grads = jnp.stack(parts, 0)
    gate_grad = grads[:, :, :, 0].transpose(2, 1, 0, 3).reshape(512, 1024)
    up_grad = grads[:, :, :, 1].transpose(2, 1, 0, 3).reshape(512, 1024)

    def input_part(d):
        total = None
        for k in range(CHUNKS):
            pieces = weights[k][d]
            term = [dot(deltas[k], piece, 1, 1) for piece in pieces]
            term = term[0] if len(term) == 1 else jnp.concatenate(term, 1)
            total = term if total is None else total + term
        return total.astype(bf)

    def input_half(ds):
        half = jnp.concatenate([input_part(d) for d in ds], 1)
        return half.reshape(2, 2, 2, 2, 2, 32, 2048)

    first = scatter_sum(
        input_half((0, 1)), [(CORE, c, 0), (ZBOTH, zh, 0), (ZLO, zl, 0), (YBOTH, yh, 0), (YLO, yl, 0)]
    )
    second = scatter_sum(
        input_half((2, 3)), [(CORE, c, 0), (YBOTH, yh, 2), (YLO, yl, 2), (ZBOTH, zh, 0), (ZLO, zl, 0)]
    )
    rolled = jnp.concatenate([first, second], 1).reshape(32, 4, 1024)
    input_grad = jnp.take(rolled, (jnp.arange(4) - x) % 4, axis=1).reshape(32, 4096)
    return input_grad, gate_grad, up_grad


def solution(mesh):
    in_specs = (
        P(("node", "local"), None),
        P("node", "local"),
        P("node", "local"),
        P("node", "local"),
    )
    out_specs = (P(("node", "local"), None), P("node", "local"), P("node", "local"))
    return jax.shard_map(shards, mesh=mesh, in_specs=in_specs, out_specs=out_specs, check_vma=False)
```

```python
import functools

import jax
import jax.numpy as jnp
from jax import lax
from jax.experimental import pallas as pl
from jax.experimental.pallas import tpu as pltpu
from jax.sharding import PartitionSpec as P

AXES = ("node", "local")
BF, F32 = jnp.bfloat16, jnp.float32
MIB = 1 << 20


def place(i):
    n, l = divmod(i, 16)
    return (n // 2, n % 2, l // 4, (l // 2) % 2, l % 2)


def index(x, yl, z, yh, c):
    return (x * 2 + yl) * 16 + z * 4 + yh * 2 + c


def pairs(move):
    return [(i, index(*move(*place(i)))) for i in range(128)]


LINKS = {
    "u": lambda x, yl, z, yh, c: (x, 1 - yl, z, yh, c),
    "v": lambda x, yl, z, yh, c: (x, 1 - yl, z, 1 - yh, c),
    "p": lambda x, yl, z, yh, c: (x, yl, z ^ 1, yh, c),
    "q": lambda x, yl, z, yh, c: (x, yl, 3 - z, yh, c),
}
XUP = pairs(lambda x, yl, z, yh, c: ((x + 1) % 4, yl, z, yh, c))
XDOWN = pairs(lambda x, yl, z, yh, c: ((x + 3) % 4, yl, z, yh, c))
YLO = pairs(LINKS["u"])
CORE = pairs(lambda x, yl, z, yh, c: (x, yl, z, yh, 1 - c))
ORDERS = (("uvpq", "pquv"), ("vuqp", "qpvu"))
WEIGHT = {"q": 8, "p": 4, "v": 2, "u": 1}


def both_cores(link0, link1):
    return pairs(lambda *at: LINKS[link1 if at[4] else link0](*at))


def send(value, to):
    return lax.ppermute(value, AXES, to)


def after(value, *others):
    return lax.optimization_barrier((value, *others))[0]


def pick(value, at):
    return lax.dynamic_index_in_dim(value, at, 0, keepdims=False)


def join(own, other, bit):
    where = lax.broadcasted_iota(jnp.int32, (2,) + own.shape, 0) == bit
    both = jnp.where(where, own[None], other[None])
    return both.reshape((2 * own.shape[0],) + own.shape[1:])


def cost(bytes_):
    return pl.CostEstimate(flops=1, bytes_accessed=bytes_ // 64, transcendentals=0)


def params(mib=24):
    return pltpu.CompilerParams(vmem_limit_bytes=mib * MIB)


def shape(rows, columns, kind=BF):
    return jax.ShapeDtypeStruct((rows, columns), kind)


def whole(rows, columns):
    return pl.BlockSpec((rows, columns), lambda *_: (0, 0))


def prep_kernel(s, x_ref, h_ref, g_ref, u_ref, keep, give, own, oth, h_own, h_oth):
    x, yl, c = s[0], s[1], s[2]
    mine, theirs = pl.multiple_of(yl * 512, 512), pl.multiple_of((1 - yl) * 512, 512)
    for base, out in ((mine, own), (theirs, oth)):
        out[:, :512] = g_ref[:, pl.ds(base, 512)]
        out[:, 512:] = u_ref[:, pl.ds(base, 512)]
    h_own[...] = h_ref[:, pl.ds(mine, 512)]
    h_oth[...] = h_ref[:, pl.ds(theirs, 512)]

    @pl.when(pl.program_id(0) == 0)
    def _():
        for d in range(4):
            base = lax.rem(x + d, 4) * 1024
            for out, half in ((keep, c), (give, 1 - c)):
                out[:, d * 512 : (d + 1) * 512] = x_ref[
                    :, pl.ds(pl.multiple_of(base + half * 512, 512), 512)
                ]


def prep(scalars, inputs, hidden_grad, w_gate, w_up):
    rows = lambda columns: pl.BlockSpec((128, columns), lambda i, s: (i, 0))
    return pl.pallas_call(
        prep_kernel,
        grid_spec=pltpu.PrefetchScalarGridSpec(
            num_scalar_prefetch=1,
            grid=(4,),
            in_specs=[whole(32, 4096), rows(1024), rows(1024), rows(1024)],
            out_specs=[whole(32, 2048)] * 2 + [rows(1024)] * 2 + [rows(512)] * 2,
        ),
        out_shape=[shape(32, 2048)] * 2 + [shape(512, 1024)] * 2 + [shape(512, 512)] * 2,
        compiler_params=params(),
        cost_estimate=cost(6 * MIB),
        name="prep",
    )(scalars, inputs, hidden_grad, w_gate, w_up)


def arrange_kernel(place_of, s, own, other, out):
    for which, source in enumerate((own, other)):
        for sub in range(8):
            to = pl.multiple_of(place_of(s, which, sub) * 64, 64)
            out[pl.ds(to, 64), :] = source[sub * 64 : (sub + 1) * 64, :]


def arrange(scalars, own, other, place_of, name):
    columns = own.shape[1]
    spec = lambda rows: pl.BlockSpec((rows, 256), lambda i, s: (0, i))
    return pl.pallas_call(
        functools.partial(arrange_kernel, place_of),
        grid_spec=pltpu.PrefetchScalarGridSpec(
            num_scalar_prefetch=1,
            grid=(columns // 256,),
            in_specs=[spec(512)] * 2,
            out_specs=spec(1024),
        ),
        out_shape=shape(1024, columns),
        compiler_params=params(),
        cost_estimate=cost(4 * 1024 * columns),
        name=name,
    )(scalars, own, other)


def token_place(j, s, which, sub):
    c = s[2]
    bits = (None, (sub >> 2) & 1, (sub >> 1) & 1, sub & 1)
    at = []
    for core in range(2):
        order = ORDERS[j][core][::-1]
        mine = s[{"q": 3, "p": 4, "v": 5, "u": 6}[order[0]]]
        last = mine if which == 0 else 1 - mine
        at.append(
            last * WEIGHT[order[0]] + sum(bits[n] * WEIGHT[order[n]] for n in range(1, 4))
        )
    return jnp.where(c == 0, at[0], at[1])


def hidden_place(s, which, sub):
    yl = s[1] if which == 0 else 1 - s[1]
    zh, zl, yh = (sub >> 2) & 1, (sub >> 1) & 1, sub & 1
    u = 1 - yl if yh else yl
    return zh * 8 + (zl ^ zh) * 4 + yh * 2 + u


def gate_sum(spans, mine, s, refs):
    count = max(block for block, _, _ in spans) + 1
    own_now = (s[1] == s[2]) if mine else (s[1] != s[2])
    tokens = [jnp.where(own_now, refs[n][...], refs[count + n][...]) for n in range(count)]
    acc = None
    for (block, at, rows), piece in zip(spans, refs[2 * count :]):
        term = jnp.dot(tokens[block][:, at : at + rows], piece[...], preferred_element_type=F32)
        acc = term if acc is None else acc + term
    return acc


def gate_own(s, *refs):
    refs[-1][...] = gate_sum(OWN_SPANS, True, s, refs)


def gate_other(s, *refs):
    refs[-1][...] = refs[-2][...] + gate_sum(OTHER_SPANS, False, s, refs)


def gate_far(s, *refs):
    partial, hidden, delta = refs[-3:]
    total = partial[...] + gate_sum(FAR_SPANS, False, s, refs)
    gate, upper = total[:, :512], total[:, 512:]
    sigma = 1.0 / (1.0 + jnp.exp(-gate))
    grad = hidden[...].astype(F32)
    delta[:, :512] = (grad * upper * sigma * (1.0 + gate * (1.0 - sigma))).astype(BF)
    delta[:, 512:] = (grad * gate * sigma).astype(BF)


OWN_SPANS = ((0, 0, 512), (1, 0, 512), (2, 0, 256), (2, 256, 256), (3, 0, 512))
OTHER_SPANS = ((0, 0, 256), (0, 256, 256), (1, 0, 256), (1, 256, 256), (2, 0, 256), (2, 256, 256))
FAR_SPANS = ((0, 0, 256), (0, 256, 256))
TILE = 256


def rows_of(columns, at=0):
    return pl.BlockSpec((TILE, columns), lambda i, s: (i, at))


def gate_call(kernel, scalars, tokens, blocks, pieces, more, out, name):
    picked = [(tokens[2 * side + d // 2], d % 2) for side in range(2) for d in blocks]
    return pl.pallas_call(
        kernel,
        grid_spec=pltpu.PrefetchScalarGridSpec(
            num_scalar_prefetch=1,
            grid=(1024 // TILE,),
            in_specs=[rows_of(512, at) for _, at in picked]
            + [whole(*piece.shape) for piece in pieces]
            + [rows_of(array.shape[1]) for array in more],
            out_specs=rows_of(1024),
        ),
        out_shape=shape(1024, 1024, out),
        compiler_params=params(),
        cost_estimate=cost(14 * MIB),
        name=name,
    )(scalars, *[array for array, _ in picked], *pieces, *more)


def grads_call(blocks, delta, kind, halved, name):
    count = len(blocks)
    at = [half for _, half in blocks]
    parts = [(n, start, 256) for n in range(halved) for start in (0, 256)]
    parts += [(n, 0, 512) for n in range(halved, count)]

    def kernel(*refs):
        columns, delta_in = refs[:count], refs[count]
        outs = refs[count + 1 : count + 1 + len(parts)]
        tokens, deltas, results, in_sems, out_sems = refs[count + 1 + len(parts) :]
        loads = [pltpu.make_async_copy(delta_in, deltas, in_sems.at[count])]
        for n in range(count):
            source = columns[n].at[:, pl.ds(at[n] * 512, 512)]
            loads.append(pltpu.make_async_copy(source, tokens.at[n], in_sems.at[n]))
        for load in loads:
            load.start()
        loads[0].wait()
        stores = []
        for n in range(count):
            loads[n + 1].wait()
            results[n] = lax.dot_general(
                tokens[n], deltas[...], (((0,), (0,)), ((), ())), preferred_element_type=F32
            ).astype(kind)
            for m, (which, start, rows) in enumerate(parts):
                if which == n:
                    source = results.at[n, pl.ds(start, rows)]
                    stores.append(pltpu.make_async_copy(source, outs[m], out_sems.at[m]))
                    stores[-1].start()
        for store in stores:
            store.wait()

    return pl.pallas_call(
        kernel,
        in_specs=[pl.BlockSpec(memory_space=pl.ANY)] * (count + 1),
        out_specs=[pl.BlockSpec(memory_space=pl.ANY)] * len(parts),
        out_shape=[shape(rows, 1024, kind) for _, _, rows in parts],
        scratch_shapes=[
            pltpu.VMEM((count, 1024, 512), BF),
            pltpu.VMEM((1024, 1024), BF),
            pltpu.VMEM((count, 512, 1024), kind),
            pltpu.SemaphoreType.DMA((count + 1,)),
            pltpu.SemaphoreType.DMA((len(parts),)),
        ],
        compiler_params=params(),
        cost_estimate=cost(10 * MIB),
        name=name,
    )(*[array for array, _ in blocks], delta)


def igrad_call(scalars, j, delta, mine, theirs):
    flat = [(array, which, d, at) for which, group in enumerate((mine, theirs))
            for d in range(2) for at, array in enumerate(group[d])]
    count = len(flat)

    def kernel(s, *refs):
        delta_in, arrays = refs[0], refs[1 : count + 1]
        own_out, rec_out = refs[count + 1 : count + 3]
        deltas, pieces, results, in_sems, out_sems = refs[count + 3 :]
        c = s[2]
        loads = [pltpu.make_async_copy(delta_in, deltas, in_sems.at[count])]
        for n, (array, which, d, at) in enumerate(flat):
            rows = array.shape[0]
            target = pieces.at[which, d, pl.ds(at * rows, rows)]
            loads.append(pltpu.make_async_copy(arrays[n], target, in_sems.at[n]))
        for load in loads:
            load.start()
        loads[0].wait()
        side = jnp.where(s[1] == c, 1, 0)
        stores = []
        for d in range(2):
            for n in range(count):
                if flat[n][2] == d:
                    loads[n + 1].wait()
            for turn, (out, which, core) in enumerate(
                ((rec_out, side, 1 - c), (own_out, 1 - side, c))
            ):
                columns = slice(d * 512, (d + 1) * 512)
                piece = pieces[which, d]
                for block in range(16):
                    if block % 4 == 0:
                        acc = lax.dot_general(
                            deltas[block * 64 : block * 64 + 256],
                            piece,
                            (((1,), (1,)), ((), ())),
                            preferred_element_type=F32,
                        ).astype(BF)
                    bits = {link: (block // weight) % 2 for link, weight in WEIGHT.items()}
                    at = [sum(bits[l] << n for n, l in enumerate(order)) for order in ORDERS[j]]
                    to = pl.multiple_of(jnp.where(core == 0, at[0], at[1]) * 64, 64)
                    part = (block % 4) * 64
                    results[turn, pl.ds(to, 64), columns] = acc[part : part + 64]
                stores.append(
                    pltpu.make_async_copy(
                        results.at[turn, :, columns], out.at[:, columns], out_sems.at[turn, d]
                    )
                )
                stores[-1].start()
        for store in stores:
            store.wait()

    return pl.pallas_call(
        kernel,
        grid_spec=pltpu.PrefetchScalarGridSpec(
            num_scalar_prefetch=1,
            grid=(),
            in_specs=[pl.BlockSpec(memory_space=pl.ANY)] * (count + 1),
            out_specs=[pl.BlockSpec(memory_space=pl.ANY)] * 2,
            scratch_shapes=[
                pltpu.VMEM((1024, 1024), BF),
                pltpu.VMEM((2, 2, 512, 1024), BF),
                pltpu.VMEM((2, 1024, 1024), BF),
                pltpu.SemaphoreType.DMA((count + 1,)),
                pltpu.SemaphoreType.DMA((2, 2)),
            ],
        ),
        out_shape=[shape(1024, 1024)] * 2,
        compiler_params=params(),
        cost_estimate=cost(10 * MIB),
        name="igrad",
    )(scalars, delta, *[array for array, _, _, _ in flat])


def put_kernel(s, piece, *refs):
    gate, up = refs[-2:]
    gate[...] = piece[:, :512].astype(F32)
    up[...] = piece[:, 512:].astype(F32)


def put(scalars, half, other, piece, outs):
    column = (lambda s: 1 - s[1]) if other else (lambda s: s[1])
    return pl.pallas_call(
        put_kernel,
        grid_spec=pltpu.PrefetchScalarGridSpec(
            num_scalar_prefetch=1,
            grid=(2,),
            in_specs=[pl.BlockSpec((128, 1024), lambda i, s: (i, 0))]
            + [pl.BlockSpec(memory_space=pl.ANY)] * len(outs),
            out_specs=[pl.BlockSpec((128, 512), lambda i, s: (i + 2 * half, column(s)))] * 2,
        ),
        out_shape=[shape(512, 1024, F32)] * 2,
        input_output_aliases={2 + n: n for n in range(len(outs))},
        compiler_params=params(),
        cost_estimate=cost(3 * MIB),
        name="put",
    )(scalars, piece, *outs)


def shards(inputs, hidden_grad, w_gate, w_up):
    node, local = lax.axis_index("node"), lax.axis_index("local")
    x, yl = node // 2, node % 2
    zh, zl, yh, c = local // 8, (local // 4) % 2, (local // 2) % 2, local % 2
    bit = {"q": zh, "p": (zl + zh) % 2, "v": yh, "u": (yl + yh) % 2}
    scalars = jnp.stack([x, yl, c] + [bit[link] for link in "qpvu"]).astype(jnp.int32)
    stages = [
        [(both_cores(a, b), jnp.where(c == 0, bit[a], bit[b])) for a, b in zip(*orders)]
        for orders in ORDERS
    ]

    keep, give, own, oth, h_own, h_oth = prep(scalars, inputs, hidden_grad, w_gate, w_up)
    own_down, own_up = send(own, XUP), send(own, XDOWN)
    rows = join(keep, send(give, CORE), c)
    chains = [rows[:, :1024], rows[:, 1024:]]
    step = lambda n: [join(v, send(v, st[n][0]), st[n][1]) for v, st in zip(chains, stages)]
    chains = step(0)
    chains = step(1)
    other_a = send(after(oth[:256], *chains), YLO)
    chains = step(2)
    chains = [after(v, own_down, own_up) for v in chains]
    far_a = send(after(own_down[:256], own_up), XUP)
    far_b = send(after(own_up[256:], own_down), XDOWN)
    lasts = [send(v, st[3][0]) for v, st in zip(chains, stages)]
    other_b = send(after(oth[256:], other_a), YLO)
    lasts = [after(v, far_a, far_b, other_a) for v in lasts]
    a_down, a_up = send(after(other_a, *lasts), XUP), send(after(other_a, *lasts), XDOWN)
    own_tokens = [
        arrange(scalars, v, last, functools.partial(token_place, j), "arrange")
        for j, (v, last) in enumerate(zip(chains, lasts))
    ]
    rec_tokens = [send(block, CORE) for block in own_tokens]
    tokens = own_tokens + rec_tokens
    other_b = after(other_b, *rec_tokens)
    b_down, b_up = send(other_b, XUP), send(other_b, XDOWN)
    partial = gate_call(
        gate_own, scalars, [after(tokens[0], other_b), *tokens[1:]], (0, 1, 2, 3),
        [own, own_up, far_a, far_b, own_down], [], F32, "gate_own",
    )
    h_other = send(after(h_oth, other_b), YLO)
    a_down = after(a_down, partial)
    other_far_a = send(after(a_down, a_up), XUP)
    other_far_b = send(after(b_up, b_down, partial), XDOWN)
    hidden = arrange(scalars, h_own, h_other, hidden_place, "arrange_hidden")
    partial = gate_call(
        gate_other, scalars, [after(tokens[0], hidden), *tokens[1:]], (0, 1, 3),
        [other_a, other_b, a_up, b_up, a_down, b_down], [partial], F32, "gate_other",
    )
    delta = gate_call(
        gate_far, scalars, tokens, (2,), [other_far_a, other_far_b], [partial, hidden], BF, "gate_far",
    )
    own_pieces = [[own], [own_up], [far_a, far_b], [own_down]]
    other_pieces = [[other_a, other_b], [a_up, b_up], [other_far_a, other_far_b], [a_down, b_down]]

    block = lambda side, d: (tokens[2 * side + d // 2], d % 2)
    far_own_a, far_own_b, far_rec_a, far_rec_b, near_rec, near_own = grads_call(
        [block(0, 2), block(1, 2), block(1, 1), block(0, 3)], delta, BF, 2, "away_grads"
    )
    via_down_a, via_up_a = send(far_own_a, XUP), send(far_rec_a, XDOWN)
    via_down_b, via_up_b = send(far_own_b, XUP), send(far_rec_b, XDOWN)

    def igrad(j, order):
        return igrad_call(
            scalars, j, order, own_pieces[2 * j : 2 * j + 2], other_pieces[2 * j : 2 * j + 2]
        )

    def halve(value, stage, *deps):
        to, at = stage
        halves = value.reshape(2, -1, 1024)
        other = send(after(pick(halves, 1 - at), *deps), to)
        return (pick(halves, at).astype(F32) + other.astype(F32)).astype(BF)

    core_sum = lambda own_i, rec_i: (own_i.astype(F32) + send(rec_i, CORE).astype(F32)).astype(BF)
    own_0, rec_0 = igrad(0, after(delta, far_own_a))
    sum_0 = core_sum(own_0, rec_0)
    order = after(delta, rec_0, via_down_a, via_up_a)
    own_1, rec_1 = igrad(1, order)
    sum_1 = core_sum(own_1, after(rec_1, sum_0))
    near_down, near_up = send(after(near_rec, via_down_a), XUP), send(after(near_own, via_up_a), XDOWN)
    up_own, down_rec, home_own, home_rec = grads_call(
        [block(0, 1), block(1, 3), block(0, 0), block(1, 0)],
        after(order, rec_1, via_down_b, via_up_b), F32, 0, "home_grads",
    )
    sum_0 = halve(sum_0, stages[0][3])
    sum_1 = halve(sum_1, stages[1][3])
    add = lambda a, b: (a + b.astype(F32)).astype(BF)
    up_a, down_a = add(up_own[:256], via_down_a), add(down_rec[:256], via_up_a)
    up_b, down_b = add(up_own[256:], via_down_b), add(down_rec[256:], via_up_b)
    end_a = send(after(up_a, near_down, near_up), XUP), send(after(down_a, near_down, near_up), XDOWN)
    sum_0 = halve(sum_0, stages[0][2])
    sum_1 = halve(sum_1, stages[1][2])
    sum_0 = halve(sum_0, stages[0][1], near_down, near_up)
    sum_1 = halve(sum_1, stages[1][1], near_down, near_up)
    end_b = send(after(up_b, sum_0), XUP), send(after(down_b, sum_0), XDOWN)
    sum_0 = halve(sum_0, stages[0][0])
    sum_1 = halve(sum_1, stages[1][0])
    sums = jnp.concatenate([v.reshape(2, 32, 2, 512) for v in (sum_0, sum_1)], 2)
    kept, other = pick(sums, c), send(pick(sums, 1 - c), CORE)
    halves = jnp.where(c == 0, jnp.stack([kept, other], 2), jnp.stack([other, kept], 2))
    input_grad = jnp.take(halves.reshape(32, 4, 1024), (jnp.arange(4) - x) % 4, axis=1)

    outs, others = (), []
    for half, (end_down, end_up) in enumerate((end_a, end_b)):
        at = slice(half * 256, half * 256 + 256)
        own_sum = home_own[at] + end_down.astype(F32) + near_up[at].astype(F32)
        rec_sum = home_rec[at] + near_down[at].astype(F32) + end_up.astype(F32)
        others.append(send(jnp.where(yl == c, rec_sum, own_sum).astype(BF), YLO))
        outs = put(scalars, half, False, jnp.where(yl == c, own_sum, rec_sum), outs)
    for half, other in enumerate(others):
        outs = put(scalars, half, True, other, outs)
    return input_grad.reshape(32, 4096), *outs


def solution(mesh):
    in_specs = (
        P(("node", "local"), None),
        P("node", "local"),
        P("node", "local"),
        P("node", "local"),
    )
    out_specs = (P(("node", "local"), None), P("node", "local"), P("node", "local"))
    return jax.shard_map(shards, mesh=mesh, in_specs=in_specs, out_specs=out_specs, check_vma=False)
```

```python
import functools

import jax
import jax.numpy as jnp
from jax import lax
from jax.experimental import pallas as pl
from jax.experimental.pallas import tpu as pltpu
from jax.sharding import PartitionSpec as P

AXES = ("node", "local")
BF, F32 = jnp.bfloat16, jnp.float32
MIB = 1 << 20


def place(i):
    n, l = divmod(i, 16)
    return (n // 2, n % 2, l // 4, (l // 2) % 2, l % 2)


def index(x, yl, z, yh, c):
    return (x * 2 + yl) * 16 + z * 4 + yh * 2 + c


def pairs(move):
    return [(i, index(*move(*place(i)))) for i in range(128)]


LINKS = {
    "u": lambda x, yl, z, yh, c: (x, 1 - yl, z, yh, c),
    "v": lambda x, yl, z, yh, c: (x, 1 - yl, z, 1 - yh, c),
    "p": lambda x, yl, z, yh, c: (x, yl, z ^ 1, yh, c),
    "q": lambda x, yl, z, yh, c: (x, yl, 3 - z, yh, c),
}
XUP = pairs(lambda x, yl, z, yh, c: ((x + 1) % 4, yl, z, yh, c))
XDOWN = pairs(lambda x, yl, z, yh, c: ((x + 3) % 4, yl, z, yh, c))
YLO = pairs(LINKS["u"])
CORE = pairs(lambda x, yl, z, yh, c: (x, yl, z, yh, 1 - c))
ORDERS = (("vupq", "qvup"), ("puqv", "pqvu"))
OUT_ORDERS = (("qpvu", "pquv"), ("qvup", "vupq"))
WEIGHT = {"q": 8, "p": 4, "v": 2, "u": 1}


def both_cores(link0, link1):
    return pairs(lambda *at: LINKS[link1 if at[4] else link0](*at))


def send(value, to):
    return lax.ppermute(value, AXES, to)


def after(value, *others):
    return lax.optimization_barrier((value, *others))[0]


def pick(value, at):
    return lax.dynamic_index_in_dim(value, at, 0, keepdims=False)


def join(own, other, bit):
    where = lax.broadcasted_iota(jnp.int32, (2,) + own.shape, 0) == bit
    both = jnp.where(where, own[None], other[None])
    return both.reshape((2 * own.shape[0],) + own.shape[1:])


def cost(bytes_):
    return pl.CostEstimate(flops=1, bytes_accessed=bytes_ // 64, transcendentals=0)


def params(mib=24):
    return pltpu.CompilerParams(vmem_limit_bytes=mib * MIB)


def shape(rows, columns, kind=BF):
    return jax.ShapeDtypeStruct((rows, columns), kind)


def whole(rows, columns):
    return pl.BlockSpec((rows, columns), lambda *_: (0, 0))


def first_kernel(s, x_ref, g_ref, u_ref, keep, give, own):
    x, c = s[0], s[2]
    own[:, :512] = g_ref[...]
    own[:, 512:] = u_ref[...]

    @pl.when(pl.program_id(0) == 0)
    def _():
        for d in range(4):
            base = lax.rem(x + d, 4) * 1024
            for out, half in ((keep, c), (give, 1 - c)):
                out[:, d * 512 : (d + 1) * 512] = x_ref[
                    :, pl.ds(pl.multiple_of(base + half * 512, 512), 512)
                ]


def first_pieces(scalars, inputs, w_gate, w_up):
    rows = lambda columns: pl.BlockSpec((256, columns), lambda i, s: (i, 0))
    mine = pl.BlockSpec((256, 512), lambda i, s: (i, s[1]))
    return pl.pallas_call(
        first_kernel,
        grid_spec=pltpu.PrefetchScalarGridSpec(
            num_scalar_prefetch=1,
            grid=(2,),
            in_specs=[whole(32, 4096), mine, mine],
            out_specs=[whole(32, 2048)] * 2 + [rows(1024)],
        ),
        out_shape=[shape(32, 2048)] * 2 + [shape(512, 1024)],
        compiler_params=params(60),
        cost_estimate=cost(4 * MIB),
        name="first_pieces",
    )(scalars, inputs, w_gate, w_up)


def next_kernel(s, g_ref, u_ref, oth):
    oth[:, :512] = g_ref[...]
    oth[:, 512:] = u_ref[...]


def hidden_kernel(s, own_ref, oth_ref, own, oth):
    own[...] = own_ref[...]
    oth[...] = oth_ref[...]


def hidden_pieces(scalars, hidden_grad):
    mine = pl.BlockSpec((256, 512), lambda i, s: (i, s[1]))
    theirs = pl.BlockSpec((256, 512), lambda i, s: (i, 1 - s[1]))
    return pl.pallas_call(
        hidden_kernel,
        grid_spec=pltpu.PrefetchScalarGridSpec(
            num_scalar_prefetch=1,
            grid=(2,),
            in_specs=[mine, theirs],
            out_specs=[pl.BlockSpec((256, 512), lambda i, s: (i, 0))] * 2,
        ),
        out_shape=[shape(512, 512)] * 2,
        compiler_params=params(),
        cost_estimate=cost(2 * MIB),
        name="hidden_pieces",
    )(scalars, hidden_grad, hidden_grad)


def next_pieces(scalars, w_gate, w_up):
    theirs = pl.BlockSpec((256, 512), lambda i, s: (i, 1 - s[1]))
    return pl.pallas_call(
        next_kernel,
        grid_spec=pltpu.PrefetchScalarGridSpec(
            num_scalar_prefetch=1,
            grid=(2,),
            in_specs=[theirs, theirs],
            out_specs=pl.BlockSpec((256, 1024), lambda i, s: (i, 0)),
        ),
        out_shape=shape(512, 1024),
        compiler_params=params(60),
        cost_estimate=cost(2 * MIB),
        name="next_pieces",
    )(scalars, w_gate, w_up)


def arrange_kernel(place_of, s, own, other, out):
    for which, source in enumerate((own, other)):
        for sub in range(8):
            to = pl.multiple_of(place_of(s, which, sub) * 64, 64)
            out[pl.ds(to, 64), :] = source[sub * 64 : (sub + 1) * 64, :]


def arrange(scalars, own, other, place_of, name):
    columns = own.shape[1]
    spec = lambda rows: pl.BlockSpec((rows, 256), lambda i, s: (0, i))
    return pl.pallas_call(
        functools.partial(arrange_kernel, place_of),
        grid_spec=pltpu.PrefetchScalarGridSpec(
            num_scalar_prefetch=1,
            grid=(columns // 256,),
            in_specs=[spec(512)] * 2,
            out_specs=spec(1024),
        ),
        out_shape=shape(1024, columns),
        compiler_params=params(),
        cost_estimate=cost(4 * 1024 * columns),
        name=name,
    )(scalars, own, other)


def token_place(j, s, which, sub):
    c = s[2]
    bits = (None, (sub >> 2) & 1, (sub >> 1) & 1, sub & 1)
    at = []
    for core in range(2):
        order = ORDERS[j][core][::-1]
        mine = s[{"q": 3, "p": 4, "v": 5, "u": 6}[order[0]]]
        last = mine if which == 0 else 1 - mine
        at.append(
            last * WEIGHT[order[0]] + sum(bits[n] * WEIGHT[order[n]] for n in range(1, 4))
        )
    return jnp.where(c == 0, at[0], at[1])


def hidden_place(s, which, sub):
    yl = s[1] if which == 0 else 1 - s[1]
    zh, zl, yh = (sub >> 2) & 1, (sub >> 1) & 1, sub & 1
    u = 1 - yl if yh else yl
    return zh * 8 + (zl ^ zh) * 4 + yh * 2 + u


def gate_sum(spans, mine, s, refs):
    count = max(block for block, _, _ in spans) + 1
    own_now = (s[1] == s[2]) if mine else (s[1] != s[2])
    tokens = [jnp.where(own_now, refs[n][...], refs[count + n][...]) for n in range(count)]
    acc = None
    for (block, at, rows), piece in zip(spans, refs[2 * count :]):
        term = jnp.dot(tokens[block][:, at : at + rows], piece[...], preferred_element_type=F32)
        acc = term if acc is None else acc + term
    return acc


def gate_own(s, *refs):
    refs[-1][...] = gate_sum(OWN_SPANS, True, s, refs)


def gate_other(s, *refs):
    refs[-1][...] = refs[-2][...] + gate_sum(OTHER_SPANS, False, s, refs)


def gate_far(s, *refs):
    partial, hidden, delta = refs[-3:]
    total = partial[...] + gate_sum(FAR_SPANS, False, s, refs)
    gate, upper = total[:, :512], total[:, 512:]
    sigma = 1.0 / (1.0 + jnp.exp(-gate))
    grad = hidden[...].astype(F32)
    delta[:, :512] = (grad * upper * sigma * (1.0 + gate * (1.0 - sigma))).astype(BF)
    delta[:, 512:] = (grad * gate * sigma).astype(BF)


OWN_SPANS = ((0, 0, 512), (1, 0, 512), (2, 0, 256), (2, 256, 256), (3, 0, 512))
OTHER_SPANS = ((0, 0, 512), (1, 0, 512), (2, 0, 512))
FAR_SPANS = ((0, 0, 256), (0, 256, 256))
TILE = 256


def rows_of(columns, at=0):
    return pl.BlockSpec((TILE, columns), lambda i, s: (i, at))


def gate_call(kernel, scalars, tokens, blocks, pieces, more, out, name):
    picked = [(tokens[2 * side + d // 2], d % 2) for side in range(2) for d in blocks]
    return pl.pallas_call(
        kernel,
        grid_spec=pltpu.PrefetchScalarGridSpec(
            num_scalar_prefetch=1,
            grid=(1024 // TILE,),
            in_specs=[rows_of(512, at) for _, at in picked]
            + [whole(*piece.shape) for piece in pieces]
            + [rows_of(array.shape[1]) for array in more],
            out_specs=rows_of(1024),
        ),
        out_shape=shape(1024, 1024, out),
        compiler_params=params(),
        cost_estimate=cost(14 * MIB),
        name=name,
    )(scalars, *[array for array, _ in picked], *pieces, *more)


def grads_call(blocks, groups, delta, kind, name):
    count = len(blocks)
    parts = []
    for m, group in enumerate(groups):
        row = 0
        for n, start, rows in group:
            parts.append((n, start, rows, m, row))
            row += rows

    def kernel(*refs):
        columns, delta_in = refs[:count], refs[count]
        outs = refs[count + 1 : count + 1 + len(groups)]
        tokens, deltas, results, in_sems, out_sems = refs[count + 1 + len(groups) :]
        loads = [pltpu.make_async_copy(delta_in, deltas, in_sems.at[count])]
        for n in range(count):
            source = columns[n].at[:, pl.ds(blocks[n][1] * 512, 512)]
            loads.append(pltpu.make_async_copy(source, tokens.at[n], in_sems.at[n]))
        for load in loads:
            load.start()
        loads[0].wait()
        stores = []
        for n in range(count):
            loads[n + 1].wait()
            results[n] = lax.dot_general(
                tokens[n], deltas[...], (((0,), (0,)), ((), ())), preferred_element_type=F32
            ).astype(kind)
            for k, (which, start, rows, m, row) in enumerate(parts):
                if which == n:
                    source = results.at[n, pl.ds(start, rows)]
                    target = outs[m].at[pl.ds(row, rows)]
                    stores.append(pltpu.make_async_copy(source, target, out_sems.at[k]))
                    stores[-1].start()
        for store in stores:
            store.wait()

    return pl.pallas_call(
        kernel,
        in_specs=[pl.BlockSpec(memory_space=pl.ANY)] * (count + 1),
        out_specs=[pl.BlockSpec(memory_space=pl.ANY)] * len(groups),
        out_shape=[shape(sum(rows for _, _, rows in group), 1024, kind) for group in groups],
        scratch_shapes=[
            pltpu.VMEM((count, 1024, 512), BF),
            pltpu.VMEM((1024, 1024), BF),
            pltpu.VMEM((count, 512, 1024), kind),
            pltpu.SemaphoreType.DMA((count + 1,)),
            pltpu.SemaphoreType.DMA((len(parts),)),
        ],
        compiler_params=params(),
        cost_estimate=cost(10 * MIB),
        name=name,
    )(*[array for array, _ in blocks], delta)


def igrad_call(scalars, j, delta, mine, theirs):
    flat = [(array, which, d, at) for which, group in enumerate((mine, theirs))
            for d in range(2) for at, array in enumerate(group[d])]
    count = len(flat)

    def kernel(s, *refs):
        delta_in, arrays = refs[0], refs[1 : count + 1]
        own_out, *rec_outs = refs[count + 1 : count + 4]
        deltas, pieces, results, in_sems, out_sems = refs[count + 4 :]
        c = s[2]
        loads = [pltpu.make_async_copy(delta_in, deltas, in_sems.at[count])]
        for n, (array, which, d, at) in enumerate(flat):
            rows = array.shape[0]
            target = pieces.at[which, d, pl.ds(at * rows, rows)]
            loads.append(pltpu.make_async_copy(arrays[n], target, in_sems.at[n]))
        for load in loads:
            load.start()
        loads[0].wait()
        side = jnp.where(s[1] == c, 1, 0)
        stores = []
        for d in range(2):
            for n in range(count):
                if flat[n][2] == d:
                    loads[n + 1].wait()
            for turn, which, core in ((0, side, 1 - c), (1, 1 - side, c)):
                columns = slice(d * 512, (d + 1) * 512)
                piece = pieces[which, d]
                for block in range(16):
                    if block % 4 == 0:
                        acc = lax.dot_general(
                            deltas[block * 64 : block * 64 + 256],
                            piece,
                            (((1,), (1,)), ((), ())),
                            preferred_element_type=F32,
                        ).astype(BF)
                    bits = {link: (block // weight) % 2 for link, weight in WEIGHT.items()}
                    at = [sum(bits[l] << n for n, l in enumerate(order)) for order in OUT_ORDERS[j]]
                    to = pl.multiple_of(jnp.where(core == 0, at[0], at[1]) * 64, 64)
                    part = (block % 4) * 64
                    results[turn, pl.ds(to, 64), columns] = acc[part : part + 64]
                moves = [(results.at[1, :, columns], own_out.at[:, columns], 4 + d)]
                if turn == 0:
                    moves = [
                        (results.at[0, pl.ds(n * 512, 512), columns], rec_outs[n].at[:, columns], 2 * d + n)
                        for n in range(2)
                    ]
                for source, target, sem in moves:
                    stores.append(pltpu.make_async_copy(source, target, out_sems.at[sem]))
                    stores[-1].start()
        for store in stores:
            store.wait()

    return pl.pallas_call(
        kernel,
        grid_spec=pltpu.PrefetchScalarGridSpec(
            num_scalar_prefetch=1,
            grid=(),
            in_specs=[pl.BlockSpec(memory_space=pl.ANY)] * (count + 1),
            out_specs=[pl.BlockSpec(memory_space=pl.ANY)] * 3,
            scratch_shapes=[
                pltpu.VMEM((1024, 1024), BF),
                pltpu.VMEM((2, 2, 512, 1024), BF),
                pltpu.VMEM((2, 1024, 1024), BF),
                pltpu.SemaphoreType.DMA((count + 1,)),
                pltpu.SemaphoreType.DMA((6,)),
            ],
        ),
        out_shape=[shape(1024, 1024)] + [shape(512, 1024)] * 2,
        compiler_params=params(),
        cost_estimate=cost(10 * MIB),
        name="igrad",
    )(scalars, delta, *[array for array, _, _, _ in flat])


def put_kernel(s, piece, *refs):
    gate, up = refs[-2:]
    gate[...] = piece[:, :512].astype(F32)
    up[...] = piece[:, 512:].astype(F32)


def put(scalars, half, other, piece, outs):
    column = (lambda s: 1 - s[1]) if other else (lambda s: s[1])
    return pl.pallas_call(
        put_kernel,
        grid_spec=pltpu.PrefetchScalarGridSpec(
            num_scalar_prefetch=1,
            grid=(2,),
            in_specs=[pl.BlockSpec((128, 1024), lambda i, s: (i, 0))]
            + [pl.BlockSpec(memory_space=pl.ANY)] * len(outs),
            out_specs=[pl.BlockSpec((128, 512), lambda i, s: (i + 2 * half, column(s)))] * 2,
        ),
        out_shape=[shape(512, 1024, F32)] * 2,
        input_output_aliases={2 + n: n for n in range(len(outs))},
        compiler_params=params(),
        cost_estimate=cost(3 * MIB),
        name="put",
    )(scalars, piece, *outs)


def shards(inputs, hidden_grad, w_gate, w_up):
    node, local = lax.axis_index("node"), lax.axis_index("local")
    x, yl = node // 2, node % 2
    zh, zl, yh, c = local // 8, (local // 4) % 2, (local // 2) % 2, local % 2
    bit = {"q": zh, "p": (zl + zh) % 2, "v": yh, "u": (yl + yh) % 2}
    scalars = jnp.stack([x, yl, c] + [bit[link] for link in "qpvu"]).astype(jnp.int32)
    def stages_of(orders):
        return [
            [(both_cores(a, b), jnp.where(c == 0, bit[a], bit[b])) for a, b in zip(*pair)]
            for pair in orders
        ]

    stages = stages_of(ORDERS)

    keep, give, own = first_pieces(scalars, inputs, w_gate, w_up)
    own_down, own_up = send(own, XUP), send(own, XDOWN)
    other = send(next_pieces(scalars, after(w_gate, own), w_up), YLO)
    rows = join(keep, send(give, CORE), c)
    chains = [rows[:, :1024], rows[:, 1024:]]
    step = lambda n: [join(v, send(v, st[n][0]), st[n][1]) for v, st in zip(chains, stages)]
    chains = step(0)
    chains = step(1)
    chains = [after(v, own_down, own_up, other) for v in chains]
    chains = step(2)
    far_a = send(after(own_down[:256], own_up), XUP)
    far_b = send(after(own_up[256:], own_down), XDOWN)
    chains = [after(v, far_a, far_b) for v in chains]
    lasts = [send(v, st[3][0]) for v, st in zip(chains, stages)]
    h_own, h_oth = hidden_pieces(scalars, after(hidden_grad, own_down, own_up))
    h_other = send(after(h_oth, far_a, far_b), YLO)
    other = after(other, far_a, far_b)
    other_down, other_up = send(other, XUP), send(other, XDOWN)
    own_tokens = [
        arrange(scalars, v, last, functools.partial(token_place, j), "arrange")
        for j, (v, last) in enumerate(zip(chains, lasts))
    ]
    rec_tokens = [send(after(block, other_down, other_up), CORE) for block in own_tokens]
    tokens = own_tokens + rec_tokens
    other_far_a = send(after(other_down[:256], other_up), XUP)
    other_far_b = send(after(other_up[256:], other_down), XDOWN)
    partial = gate_call(
        gate_own, scalars, tokens, (0, 1, 2, 3), [own, own_up, far_a, far_b, own_down], [], F32,
        "gate_own",
    )
    hidden = arrange(scalars, after(h_own, partial), h_other, hidden_place, "arrange_hidden")
    partial = gate_call(
        gate_other, scalars, [after(tokens[0], hidden), *tokens[1:]], (0, 1, 3),
        [other, other_up, other_down], [partial], F32, "gate_other",
    )
    delta = gate_call(
        gate_far, scalars, tokens, (2,), [other_far_a, other_far_b], [partial, hidden], BF, "gate_far",
    )
    own_pieces = [[own], [own_up], [far_a, far_b], [own_down]]
    other_pieces = [[other], [other_up], [other_far_a, other_far_b], [other_down]]

    block = lambda side, d: (tokens[2 * side + d // 2], d % 2)
    stages = stages_of(OUT_ORDERS)

    def igrad(j, order):
        return igrad_call(
            scalars, j, order, own_pieces[2 * j : 2 * j + 2], other_pieces[2 * j : 2 * j + 2]
        )

    def core_halve(own_i, recs, stage, *deps):
        to, at = stage
        sums = [
            (own_i[n * 512 : n * 512 + 512].astype(F32) + send(rec, CORE).astype(F32)).astype(BF)
            for n, rec in enumerate(recs)
        ]
        other = send(after(jnp.where(at == 0, sums[1], sums[0]), *deps), to)
        kept = jnp.where(at == 0, sums[0], sums[1])
        return (kept.astype(F32) + other.astype(F32)).astype(BF)

    def halve(value, stage, *deps):
        to, at = stage
        halves = value.reshape(2, -1, 1024)
        other = send(after(pick(halves, 1 - at), *deps), to)
        return (pick(halves, at).astype(F32) + other.astype(F32)).astype(BF)

    full = lambda n: [(n, 0, 512)]
    plus, minus = grads_call(
        [block(0, 2), block(1, 2), block(1, 1), block(0, 3)],
        [full(0) + full(2), full(1) + full(3)], delta, BF, "away_grads",
    )
    rest_down, rest_up = send(plus, XUP), send(minus, XDOWN)
    own_0, *rec_0 = igrad(0, after(delta, plus))
    own_1, *rec_1 = igrad(1, after(delta, own_0))
    up_own, down_rec = grads_call(
        [block(0, 1), block(1, 3)], [full(0), full(1)], after(delta, own_1), F32, "pass_grads"
    )
    home_own, home_rec = grads_call(
        [block(0, 0), block(1, 0)], [full(0), full(1)], after(delta, up_own), F32, "home_grads"
    )
    sum_0 = core_halve(own_0, rec_0, stages[0][3])
    sum_1 = core_halve(own_1, rec_1, stages[1][3])
    sum_0 = halve(sum_0, stages[0][2])
    sum_1 = halve(sum_1, stages[1][2])
    sum_0 = halve(sum_0, stages[0][1])
    sum_1 = halve(sum_1, stages[1][1])
    add = lambda a, b: (a + b.astype(F32)).astype(BF)
    near_down, near_up = rest_down[512:], rest_up[512:]
    ends = [
        (
            send(add(up_own[at : at + 256], rest_down[at : at + 256]), XUP),
            send(add(down_rec[at : at + 256], rest_up[at : at + 256]), XDOWN),
        )
        for at in (0, 256)
    ]
    sum_0 = halve(sum_0, stages[0][0])
    sum_1 = halve(sum_1, stages[1][0])
    sums = jnp.concatenate([v.reshape(2, 32, 2, 512) for v in (sum_0, sum_1)], 2)
    kept, other_sums = pick(sums, c), send(pick(sums, 1 - c), CORE)
    halves = jnp.where(c == 0, jnp.stack([kept, other_sums], 2), jnp.stack([other_sums, kept], 2))
    input_grad = jnp.take(halves.reshape(32, 4, 1024), (jnp.arange(4) - x) % 4, axis=1)

    own_sum = home_own + near_up.astype(F32)
    rec_sum = home_rec + near_down.astype(F32)
    same = yl == c
    given, kept = lax.optimization_barrier(
        (jnp.where(same, rec_sum, own_sum), jnp.where(same, own_sum, rec_sum))
    )
    outs, others, last = (), [], ()
    for half, (end_down, end_up) in enumerate(ends):
        at = slice(half * 256, half * 256 + 256)
        end_down, end_up = after(end_down, *last), after(end_up, *last)
        last = (add(given[at], jnp.where(same, end_up, end_down)),)
        others.append(send(last[0], YLO))
        end = after(jnp.where(same, end_down, end_up), *last)
        outs = put(scalars, half, False, kept[at] + end.astype(F32), outs)
    for half, other in enumerate(others):
        outs = put(scalars, half, True, other, outs)
    return input_grad.reshape(32, 4096), *outs


def solution(mesh):
    in_specs = (
        P(("node", "local"), None),
        P("node", "local"),
        P("node", "local"),
        P("node", "local"),
    )
    out_specs = (P(("node", "local"), None), P("node", "local"), P("node", "local"))
    return jax.shard_map(shards, mesh=mesh, in_specs=in_specs, out_specs=out_specs, check_vma=False)
```

```python
import functools

import jax
import jax.numpy as jnp
from jax import lax
from jax.experimental import pallas as pl
from jax.experimental.pallas import tpu as pltpu
from jax.sharding import PartitionSpec as P

AXES = ("node", "local")
BF, F32 = jnp.bfloat16, jnp.float32
MIB = 1 << 20


def place(i):
    n, l = divmod(i, 16)
    return (n // 2, n % 2, l // 4, (l // 2) % 2, l % 2)


def index(x, yl, z, yh, c):
    return (x * 2 + yl) * 16 + z * 4 + yh * 2 + c


def pairs(move):
    return [(i, index(*move(*place(i)))) for i in range(128)]


LINKS = {
    "u": lambda x, yl, z, yh, c: (x, 1 - yl, z, yh, c),
    "v": lambda x, yl, z, yh, c: (x, 1 - yl, z, 1 - yh, c),
    "p": lambda x, yl, z, yh, c: (x, yl, z ^ 1, yh, c),
    "q": lambda x, yl, z, yh, c: (x, yl, 3 - z, yh, c),
}
XUP = pairs(lambda x, yl, z, yh, c: ((x + 1) % 4, yl, z, yh, c))
XDOWN = pairs(lambda x, yl, z, yh, c: ((x + 3) % 4, yl, z, yh, c))
YLO = pairs(LINKS["u"])
CORE = pairs(lambda x, yl, z, yh, c: (x, yl, z, yh, 1 - c))
ORDERS = (("vupq", "qvup"), ("puqv", "pqvu"))
OUT_ORDERS = (("qpvu", "uqpv"), ("uvqp", "upvq"))
WEIGHT = {"q": 8, "p": 4, "v": 2, "u": 1}


def both_cores(link0, link1):
    return pairs(lambda *at: LINKS[link1 if at[4] else link0](*at))


def send(value, to):
    return lax.ppermute(value, AXES, to)


def after(value, *others):
    return lax.optimization_barrier((value, *others))[0]


def pick(value, at):
    return lax.dynamic_index_in_dim(value, at, 0, keepdims=False)


def join(own, other, bit):
    where = lax.broadcasted_iota(jnp.int32, (2,) + own.shape, 0) == bit
    both = jnp.where(where, own[None], other[None])
    return both.reshape((2 * own.shape[0],) + own.shape[1:])


def cost(bytes_):
    return pl.CostEstimate(flops=1, bytes_accessed=bytes_ // 64, transcendentals=0)


def params(mib=24):
    return pltpu.CompilerParams(vmem_limit_bytes=mib * MIB)


def shape(rows, columns, kind=BF):
    return jax.ShapeDtypeStruct((rows, columns), kind)


def whole(rows, columns):
    return pl.BlockSpec((rows, columns), lambda *_: (0, 0))


def first_kernel(s, x_ref, g_ref, u_ref, keep, give, own):
    x, c = s[0], s[2]
    own[:, :512] = g_ref[...]
    own[:, 512:] = u_ref[...]

    @pl.when(pl.program_id(0) == 0)
    def _():
        for d in range(4):
            base = lax.rem(x + d, 4) * 1024
            for out, half in ((keep, c), (give, 1 - c)):
                out[:, d * 512 : (d + 1) * 512] = x_ref[
                    :, pl.ds(pl.multiple_of(base + half * 512, 512), 512)
                ]


def first_pieces(scalars, inputs, w_gate, w_up):
    rows = lambda columns: pl.BlockSpec((256, columns), lambda i, s: (i, 0))
    mine = pl.BlockSpec((256, 512), lambda i, s: (i, s[1]))
    return pl.pallas_call(
        first_kernel,
        grid_spec=pltpu.PrefetchScalarGridSpec(
            num_scalar_prefetch=1,
            grid=(2,),
            in_specs=[whole(32, 4096), mine, mine],
            out_specs=[whole(32, 2048)] * 2 + [rows(1024)],
        ),
        out_shape=[shape(32, 2048)] * 2 + [shape(512, 1024)],
        compiler_params=params(60),
        cost_estimate=cost(4 * MIB),
        name="first_pieces",
    )(scalars, inputs, w_gate, w_up)


def next_kernel(s, g_ref, u_ref, oth):
    oth[:, :512] = g_ref[...]
    oth[:, 512:] = u_ref[...]


def hidden_kernel(s, own_ref, oth_ref, own, oth):
    own[...] = own_ref[...]
    oth[...] = oth_ref[...]


def hidden_pieces(scalars, hidden_grad):
    mine = pl.BlockSpec((256, 512), lambda i, s: (i, s[1]))
    theirs = pl.BlockSpec((256, 512), lambda i, s: (i, 1 - s[1]))
    return pl.pallas_call(
        hidden_kernel,
        grid_spec=pltpu.PrefetchScalarGridSpec(
            num_scalar_prefetch=1,
            grid=(2,),
            in_specs=[mine, theirs],
            out_specs=[pl.BlockSpec((256, 512), lambda i, s: (i, 0))] * 2,
        ),
        out_shape=[shape(512, 512)] * 2,
        compiler_params=params(),
        cost_estimate=cost(2 * MIB),
        name="hidden_pieces",
    )(scalars, hidden_grad, hidden_grad)


def next_pieces(scalars, w_gate, w_up):
    theirs = pl.BlockSpec((256, 512), lambda i, s: (i, 1 - s[1]))
    return pl.pallas_call(
        next_kernel,
        grid_spec=pltpu.PrefetchScalarGridSpec(
            num_scalar_prefetch=1,
            grid=(2,),
            in_specs=[theirs, theirs],
            out_specs=pl.BlockSpec((256, 1024), lambda i, s: (i, 0)),
        ),
        out_shape=shape(512, 1024),
        compiler_params=params(60),
        cost_estimate=cost(2 * MIB),
        name="next_pieces",
    )(scalars, w_gate, w_up)


def arrange_kernel(place_of, s, own, other, out):
    for which, source in enumerate((own, other)):
        for sub in range(8):
            to = pl.multiple_of(place_of(s, which, sub) * 64, 64)
            out[pl.ds(to, 64), :] = source[sub * 64 : (sub + 1) * 64, :]


def arrange(scalars, own, other, place_of, name):
    columns = own.shape[1]
    spec = lambda rows: pl.BlockSpec((rows, 256), lambda i, s: (0, i))
    return pl.pallas_call(
        functools.partial(arrange_kernel, place_of),
        grid_spec=pltpu.PrefetchScalarGridSpec(
            num_scalar_prefetch=1,
            grid=(columns // 256,),
            in_specs=[spec(512)] * 2,
            out_specs=spec(1024),
        ),
        out_shape=shape(1024, columns),
        compiler_params=params(),
        cost_estimate=cost(4 * 1024 * columns),
        name=name,
    )(scalars, own, other)


def token_place(j, s, which, sub):
    c = s[2]
    bits = (None, (sub >> 2) & 1, (sub >> 1) & 1, sub & 1)
    at = []
    for core in range(2):
        order = ORDERS[j][core][::-1]
        mine = s[{"q": 3, "p": 4, "v": 5, "u": 6}[order[0]]]
        last = mine if which == 0 else 1 - mine
        at.append(
            last * WEIGHT[order[0]] + sum(bits[n] * WEIGHT[order[n]] for n in range(1, 4))
        )
    return jnp.where(c == 0, at[0], at[1])


def hidden_place(s, which, sub):
    yl = s[1] if which == 0 else 1 - s[1]
    zh, zl, yh = (sub >> 2) & 1, (sub >> 1) & 1, sub & 1
    u = 1 - yl if yh else yl
    return zh * 8 + (zl ^ zh) * 4 + yh * 2 + u


def gate_sum(spans, mine, s, refs):
    count = max(block for block, _, _ in spans) + 1
    own_now = (s[1] == s[2]) if mine else (s[1] != s[2])
    tokens = [jnp.where(own_now, refs[n][...], refs[count + n][...]) for n in range(count)]
    acc = None
    for (block, at, rows), piece in zip(spans, refs[2 * count :]):
        term = jnp.dot(tokens[block][:, at : at + rows], piece[...], preferred_element_type=F32)
        acc = term if acc is None else acc + term
    return acc


def gate_own(s, *refs):
    refs[-1][...] = gate_sum(OWN_SPANS, True, s, refs)


def gate_other(s, *refs):
    refs[-1][...] = refs[-2][...] + gate_sum(OTHER_SPANS, False, s, refs)


def gate_far(s, *refs):
    partial, hidden, delta = refs[-3:]
    total = partial[...] + gate_sum(FAR_SPANS, False, s, refs)
    gate, upper = total[:, :512], total[:, 512:]
    sigma = 1.0 / (1.0 + jnp.exp(-gate))
    grad = hidden[...].astype(F32)
    delta[:, :512] = (grad * upper * sigma * (1.0 + gate * (1.0 - sigma))).astype(BF)
    delta[:, 512:] = (grad * gate * sigma).astype(BF)


OWN_SPANS = ((0, 0, 512), (1, 0, 512), (2, 0, 256), (2, 256, 256), (3, 0, 512))
OTHER_SPANS = ((0, 0, 512), (1, 0, 512), (2, 0, 512))
FAR_SPANS = ((0, 0, 256), (0, 256, 256))
TILE = 256


def rows_of(columns, at=0):
    return pl.BlockSpec((TILE, columns), lambda i, s: (i, at))


def gate_call(kernel, scalars, tokens, blocks, pieces, more, out, name):
    picked = [(tokens[2 * side + d // 2], d % 2) for side in range(2) for d in blocks]
    return pl.pallas_call(
        kernel,
        grid_spec=pltpu.PrefetchScalarGridSpec(
            num_scalar_prefetch=1,
            grid=(1024 // TILE,),
            in_specs=[rows_of(512, at) for _, at in picked]
            + [whole(*piece.shape) for piece in pieces]
            + [rows_of(array.shape[1]) for array in more],
            out_specs=rows_of(1024),
        ),
        out_shape=shape(1024, 1024, out),
        compiler_params=params(),
        cost_estimate=cost(14 * MIB),
        name=name,
    )(scalars, *[array for array, _ in picked], *pieces, *more)


def grads_call(blocks, groups, delta, kind, name):
    count = len(blocks)
    parts = []
    for m, group in enumerate(groups):
        row = 0
        for n, start, rows in group:
            parts.append((n, start, rows, m, row))
            row += rows

    def kernel(*refs):
        columns, delta_in = refs[:count], refs[count]
        outs = refs[count + 1 : count + 1 + len(groups)]
        tokens, deltas, results, in_sems, out_sems = refs[count + 1 + len(groups) :]
        loads = [pltpu.make_async_copy(delta_in, deltas, in_sems.at[count])]
        for n in range(count):
            source = columns[n].at[:, pl.ds(blocks[n][1] * 512, 512)]
            loads.append(pltpu.make_async_copy(source, tokens.at[n], in_sems.at[n]))
        for load in loads:
            load.start()
        loads[0].wait()
        stores = []
        for n in range(count):
            loads[n + 1].wait()
            results[n] = lax.dot_general(
                tokens[n], deltas[...], (((0,), (0,)), ((), ())), preferred_element_type=F32
            ).astype(kind)
            for k, (which, start, rows, m, row) in enumerate(parts):
                if which == n:
                    source = results.at[n, pl.ds(start, rows)]
                    target = outs[m].at[pl.ds(row, rows)]
                    stores.append(pltpu.make_async_copy(source, target, out_sems.at[k]))
                    stores[-1].start()
        for store in stores:
            store.wait()

    return pl.pallas_call(
        kernel,
        in_specs=[pl.BlockSpec(memory_space=pl.ANY)] * (count + 1),
        out_specs=[pl.BlockSpec(memory_space=pl.ANY)] * len(groups),
        out_shape=[shape(sum(rows for _, _, rows in group), 1024, kind) for group in groups],
        scratch_shapes=[
            pltpu.VMEM((count, 1024, 512), BF),
            pltpu.VMEM((1024, 1024), BF),
            pltpu.VMEM((count, 512, 1024), kind),
            pltpu.SemaphoreType.DMA((count + 1,)),
            pltpu.SemaphoreType.DMA((len(parts),)),
        ],
        compiler_params=params(),
        cost_estimate=cost(10 * MIB),
        name=name,
    )(*[array for array, _ in blocks], delta)


def igrad_call(scalars, j, delta, mine, theirs):
    flat = [(array, which, d, at) for which, group in enumerate((mine, theirs))
            for d in range(2) for at, array in enumerate(group[d])]
    count = len(flat)

    def kernel(s, *refs):
        delta_in, arrays = refs[0], refs[1 : count + 1]
        own_out, *rec_outs = refs[count + 1 : count + 4]
        deltas, pieces, results, in_sems, out_sems = refs[count + 4 :]
        c = s[2]
        loads = [pltpu.make_async_copy(delta_in, deltas, in_sems.at[count])]
        for n, (array, which, d, at) in enumerate(flat):
            rows = array.shape[0]
            target = pieces.at[which, d, pl.ds(at * rows, rows)]
            loads.append(pltpu.make_async_copy(arrays[n], target, in_sems.at[n]))
        for load in loads:
            load.start()
        loads[0].wait()
        side = jnp.where(s[1] == c, 1, 0)
        stores = []
        for d in range(2):
            for n in range(count):
                if flat[n][2] == d:
                    loads[n + 1].wait()
            for turn, which, core in ((0, side, 1 - c), (1, 1 - side, c)):
                columns = slice(d * 512, (d + 1) * 512)
                piece = pieces[which, d]
                for block in range(16):
                    if block % 4 == 0:
                        acc = lax.dot_general(
                            deltas[block * 64 : block * 64 + 256],
                            piece,
                            (((1,), (1,)), ((), ())),
                            preferred_element_type=F32,
                        ).astype(BF)
                    bits = {link: (block // weight) % 2 for link, weight in WEIGHT.items()}
                    at = [sum(bits[l] << n for n, l in enumerate(order)) for order in OUT_ORDERS[j]]
                    to = pl.multiple_of(jnp.where(core == 0, at[0], at[1]) * 64, 64)
                    part = (block % 4) * 64
                    results[turn, pl.ds(to, 64), columns] = acc[part : part + 64]
                moves = [(results.at[1, :, columns], own_out.at[:, columns], 4 + d)]
                if turn == 0:
                    moves = [
                        (results.at[0, pl.ds(n * 512, 512), columns], rec_outs[n].at[:, columns], 2 * d + n)
                        for n in range(2)
                    ]
                for source, target, sem in moves:
                    stores.append(pltpu.make_async_copy(source, target, out_sems.at[sem]))
                    stores[-1].start()
        for store in stores:
            store.wait()

    return pl.pallas_call(
        kernel,
        grid_spec=pltpu.PrefetchScalarGridSpec(
            num_scalar_prefetch=1,
            grid=(),
            in_specs=[pl.BlockSpec(memory_space=pl.ANY)] * (count + 1),
            out_specs=[pl.BlockSpec(memory_space=pl.ANY)] * 3,
            scratch_shapes=[
                pltpu.VMEM((1024, 1024), BF),
                pltpu.VMEM((2, 2, 512, 1024), BF),
                pltpu.VMEM((2, 1024, 1024), BF),
                pltpu.SemaphoreType.DMA((count + 1,)),
                pltpu.SemaphoreType.DMA((6,)),
            ],
        ),
        out_shape=[shape(1024, 1024)] + [shape(512, 1024)] * 2,
        compiler_params=params(),
        cost_estimate=cost(10 * MIB),
        name="igrad",
    )(scalars, delta, *[array for array, _, _, _ in flat])


def put_kernel(s, piece, *refs):
    gate, up = refs[-2:]
    gate[...] = piece[:, :512].astype(F32)
    up[...] = piece[:, 512:].astype(F32)


def put(scalars, half, other, piece, outs):
    column = (lambda s: 1 - s[1]) if other else (lambda s: s[1])
    return pl.pallas_call(
        put_kernel,
        grid_spec=pltpu.PrefetchScalarGridSpec(
            num_scalar_prefetch=1,
            grid=(2,),
            in_specs=[pl.BlockSpec((128, 1024), lambda i, s: (i, 0))]
            + [pl.BlockSpec(memory_space=pl.ANY)] * len(outs),
            out_specs=[pl.BlockSpec((128, 512), lambda i, s: (i + 2 * half, column(s)))] * 2,
        ),
        out_shape=[shape(512, 1024, F32)] * 2,
        input_output_aliases={2 + n: n for n in range(len(outs))},
        compiler_params=params(),
        cost_estimate=cost(3 * MIB),
        name="put",
    )(scalars, piece, *outs)


def shards(inputs, hidden_grad, w_gate, w_up):
    node, local = lax.axis_index("node"), lax.axis_index("local")
    x, yl = node // 2, node % 2
    zh, zl, yh, c = local // 8, (local // 4) % 2, (local // 2) % 2, local % 2
    bit = {"q": zh, "p": (zl + zh) % 2, "v": yh, "u": (yl + yh) % 2}
    scalars = jnp.stack([x, yl, c] + [bit[link] for link in "qpvu"]).astype(jnp.int32)
    def stages_of(orders):
        return [
            [(both_cores(a, b), jnp.where(c == 0, bit[a], bit[b])) for a, b in zip(*pair)]
            for pair in orders
        ]

    stages = stages_of(ORDERS)

    keep, give, own = first_pieces(scalars, inputs, w_gate, w_up)
    own_down, own_up = send(own, XUP), send(own, XDOWN)
    other = send(next_pieces(scalars, after(w_gate, own), w_up), YLO)
    rows = join(keep, send(give, CORE), c)
    chains = [rows[:, :1024], rows[:, 1024:]]
    step = lambda n: [join(v, send(v, st[n][0]), st[n][1]) for v, st in zip(chains, stages)]
    chains = step(0)
    chains = step(1)
    chains = [after(v, own_down, own_up, other) for v in chains]
    chains = step(2)
    far_a = send(after(own_down[:256], own_up), XUP)
    far_b = send(after(own_up[256:], own_down), XDOWN)
    chains = [after(v, far_a, far_b) for v in chains]
    lasts = [send(v, st[3][0]) for v, st in zip(chains, stages)]
    h_own, h_oth = hidden_pieces(scalars, after(hidden_grad, own_down, own_up))
    h_other = send(after(h_oth, far_a, far_b), YLO)
    other = after(other, far_a, far_b)
    other_down, other_up = send(other, XUP), send(other, XDOWN)
    own_tokens = [
        arrange(scalars, v, last, functools.partial(token_place, j), "arrange")
        for j, (v, last) in enumerate(zip(chains, lasts))
    ]
    rec_tokens = [send(after(block, other_down, other_up), CORE) for block in own_tokens]
    tokens = own_tokens + rec_tokens
    other_far_a = send(after(other_down[:256], other_up), XUP)
    other_far_b = send(after(other_up[256:], other_down), XDOWN)
    partial = gate_call(
        gate_own, scalars, tokens, (0, 1, 2, 3), [own, own_up, far_a, far_b, own_down], [], F32,
        "gate_own",
    )
    hidden = arrange(scalars, after(h_own, partial), h_other, hidden_place, "arrange_hidden")
    partial = gate_call(
        gate_other, scalars, [after(tokens[0], hidden, other_far_a, other_far_b), *tokens[1:]], (0, 1, 3),
        [other, other_up, other_down], [partial], F32, "gate_other",
    )
    delta = gate_call(
        gate_far, scalars, tokens, (2,), [other_far_a, other_far_b], [partial, hidden], BF, "gate_far",
    )
    own_pieces = [[own], [own_up], [far_a, far_b], [own_down]]
    other_pieces = [[other], [other_up], [other_far_a, other_far_b], [other_down]]

    block = lambda side, d: (tokens[2 * side + d // 2], d % 2)
    stages = stages_of(OUT_ORDERS)

    def igrad(j, order):
        return igrad_call(
            scalars, j, order, own_pieces[2 * j : 2 * j + 2], other_pieces[2 * j : 2 * j + 2]
        )

    def core_halve(own_i, recs, stage, *deps):
        to, at = stage
        sums = [
            (own_i[n * 512 : n * 512 + 512].astype(F32) + send(rec, CORE).astype(F32)).astype(BF)
            for n, rec in enumerate(recs)
        ]
        other = send(after(jnp.where(at == 0, sums[1], sums[0]), *deps), to)
        kept = jnp.where(at == 0, sums[0], sums[1])
        return (kept.astype(F32) + other.astype(F32)).astype(BF)

    def halve(value, stage, *deps):
        to, at = stage
        halves = value.reshape(2, -1, 1024)
        other = send(after(pick(halves, 1 - at), *deps), to)
        return (pick(halves, at).astype(F32) + other.astype(F32)).astype(BF)

    full = lambda n: [(n, 0, 512)]
    plus, minus = grads_call(
        [block(0, 2), block(1, 2), block(1, 1), block(0, 3)],
        [full(0) + full(2), full(1) + full(3)], delta, BF, "away_grads",
    )
    rest_down, rest_up = send(plus, XUP), send(minus, XDOWN)
    own_0, *rec_0 = igrad(0, after(delta, plus))
    own_1, *rec_1 = igrad(1, after(delta, own_0))
    up_own, down_rec = grads_call(
        [block(0, 1), block(1, 3)], [full(0), full(1)], after(delta, own_1), F32, "pass_grads"
    )
    home_own, home_rec = grads_call(
        [block(0, 0), block(1, 0)], [full(0), full(1)], after(delta, up_own), F32, "home_grads"
    )
    sum_0 = core_halve(own_0, rec_0, stages[0][3], rest_down, rest_up)
    sum_1 = core_halve(own_1, rec_1, stages[1][3], rest_down, rest_up)
    sum_0 = halve(sum_0, stages[0][2])
    sum_1 = halve(sum_1, stages[1][2])
    sum_0 = halve(sum_0, stages[0][1])
    sum_1 = halve(sum_1, stages[1][1])
    add = lambda a, b: (a + b.astype(F32)).astype(BF)
    passed = [
        (add(up_own[at : at + 256], rest_down[at : at + 256]), add(down_rec[at : at + 256], rest_up[at : at + 256]))
        for at in (0, 256)
    ]
    ends = [(send(passed[0][0], XUP), send(passed[0][1], XDOWN))]
    up, down = lax.optimization_barrier((*passed[1], *ends[0]))[:2]
    ends.append((send(up, XUP), send(down, XDOWN)))
    near_down, near_up = after(rest_down, *passed[1])[512:], after(rest_up, *passed[1])[512:]
    sum_0 = halve(sum_0, stages[0][0])
    sum_1 = halve(sum_1, stages[1][0])
    sums = jnp.concatenate([v.reshape(2, 32, 2, 512) for v in (sum_0, sum_1)], 2)
    kept, other_sums = pick(sums, c), send(pick(sums, 1 - c), CORE)
    halves = jnp.where(c == 0, jnp.stack([kept, other_sums], 2), jnp.stack([other_sums, kept], 2))
    input_grad = jnp.take(halves.reshape(32, 4, 1024), (jnp.arange(4) - x) % 4, axis=1)

    own_sum = home_own + near_up.astype(F32)
    rec_sum = home_rec + near_down.astype(F32)
    same = yl == c
    given, kept = lax.optimization_barrier(
        (jnp.where(same, rec_sum, own_sum), jnp.where(same, own_sum, rec_sum))
    )
    outs, others, last = (), [], ()
    for half, (end_down, end_up) in enumerate(ends):
        at = slice(half * 256, half * 256 + 256)
        end_down, end_up = after(end_down, *last), after(end_up, *last)
        last = (add(given[at], jnp.where(same, end_up, end_down)),)
        others.append(send(last[0], YLO))
        end = after(jnp.where(same, end_down, end_up), *last)
        outs = put(scalars, half, False, kept[at] + end.astype(F32), outs)
    for half, other in enumerate(others):
        outs = put(scalars, half, True, other, outs)
    return input_grad.reshape(32, 4096), *outs


def solution(mesh):
    in_specs = (
        P(("node", "local"), None),
        P("node", "local"),
        P("node", "local"),
        P("node", "local"),
    )
    out_specs = (P(("node", "local"), None), P("node", "local"), P("node", "local"))
    return jax.shard_map(shards, mesh=mesh, in_specs=in_specs, out_specs=out_specs, check_vma=False)
```

```python
import functools

import jax
import jax.numpy as jnp
from jax import lax
from jax.experimental import pallas as pl
from jax.experimental.pallas import tpu as pltpu
from jax.sharding import PartitionSpec as P

AXES = ("node", "local")
BF, F32 = jnp.bfloat16, jnp.float32
MIB = 1 << 20


def place(i):
    n, l = divmod(i, 16)
    return (n // 2, n % 2, l // 4, (l // 2) % 2, l % 2)


def index(x, yl, z, yh, c):
    return (x * 2 + yl) * 16 + z * 4 + yh * 2 + c


def pairs(move):
    return [(i, index(*move(*place(i)))) for i in range(128)]


LINKS = {
    "u": lambda x, yl, z, yh, c: (x, 1 - yl, z, yh, c),
    "v": lambda x, yl, z, yh, c: (x, 1 - yl, z, 1 - yh, c),
    "p": lambda x, yl, z, yh, c: (x, yl, z ^ 1, yh, c),
    "q": lambda x, yl, z, yh, c: (x, yl, 3 - z, yh, c),
}
XUP = pairs(lambda x, yl, z, yh, c: ((x + 1) % 4, yl, z, yh, c))
XDOWN = pairs(lambda x, yl, z, yh, c: ((x + 3) % 4, yl, z, yh, c))
YLO = pairs(LINKS["u"])
CORE = pairs(lambda x, yl, z, yh, c: (x, yl, z, yh, 1 - c))
ORDERS = (("vupq", "qvup"), ("puqv", "pqvu"))
OUT_ORDERS = (("qpvu", "uqpv"), ("uvqp", "upvq"))
WEIGHT = {"q": 8, "p": 4, "v": 2, "u": 1}


def both_cores(link0, link1):
    return pairs(lambda *at: LINKS[link1 if at[4] else link0](*at))


def send(value, to):
    return lax.ppermute(value, AXES, to)


def after(value, *others):
    return lax.optimization_barrier((value, *others))[0]


def pick(value, at):
    return lax.dynamic_index_in_dim(value, at, 0, keepdims=False)


def join(own, other, bit):
    where = lax.broadcasted_iota(jnp.int32, (2,) + own.shape, 0) == bit
    both = jnp.where(where, own[None], other[None])
    return both.reshape((2 * own.shape[0],) + own.shape[1:])


def cost(bytes_):
    return pl.CostEstimate(flops=1, bytes_accessed=bytes_ // 64, transcendentals=0)


def params(mib=24):
    return pltpu.CompilerParams(vmem_limit_bytes=mib * MIB)


def shape(rows, columns, kind=BF):
    return jax.ShapeDtypeStruct((rows, columns), kind)


def whole(rows, columns):
    return pl.BlockSpec((rows, columns), lambda *_: (0, 0))


def first_kernel(s, x_ref, g_ref, u_ref, keep, give, own):
    x, c = s[0], s[2]
    own[:, :512] = g_ref[...]
    own[:, 512:] = u_ref[...]

    @pl.when(pl.program_id(0) == 0)
    def _():
        for d in range(4):
            base = lax.rem(x + d, 4) * 1024
            for out, half in ((keep, c), (give, 1 - c)):
                out[:, d * 512 : (d + 1) * 512] = x_ref[
                    :, pl.ds(pl.multiple_of(base + half * 512, 512), 512)
                ]


def first_pieces(scalars, inputs, w_gate, w_up):
    rows = lambda columns: pl.BlockSpec((256, columns), lambda i, s: (i, 0))
    mine = pl.BlockSpec((256, 512), lambda i, s: (i, s[1]))
    return pl.pallas_call(
        first_kernel,
        grid_spec=pltpu.PrefetchScalarGridSpec(
            num_scalar_prefetch=1,
            grid=(2,),
            in_specs=[whole(32, 4096), mine, mine],
            out_specs=[whole(32, 2048)] * 2 + [rows(1024)],
        ),
        out_shape=[shape(32, 2048)] * 2 + [shape(512, 1024)],
        compiler_params=params(60),
        cost_estimate=cost(4 * MIB),
        name="first_pieces",
    )(scalars, inputs, w_gate, w_up)


def next_kernel(s, g_ref, u_ref, oth):
    oth[:, :512] = g_ref[...]
    oth[:, 512:] = u_ref[...]


def hidden_kernel(s, own_ref, oth_ref, own, oth):
    own[...] = own_ref[...]
    oth[...] = oth_ref[...]


def hidden_pieces(scalars, hidden_grad):
    mine = pl.BlockSpec((256, 512), lambda i, s: (i, s[1]))
    theirs = pl.BlockSpec((256, 512), lambda i, s: (i, 1 - s[1]))
    return pl.pallas_call(
        hidden_kernel,
        grid_spec=pltpu.PrefetchScalarGridSpec(
            num_scalar_prefetch=1,
            grid=(2,),
            in_specs=[mine, theirs],
            out_specs=[pl.BlockSpec((256, 512), lambda i, s: (i, 0))] * 2,
        ),
        out_shape=[shape(512, 512)] * 2,
        compiler_params=params(),
        cost_estimate=cost(2 * MIB),
        name="hidden_pieces",
    )(scalars, hidden_grad, hidden_grad)


def next_pieces(scalars, w_gate, w_up):
    theirs = pl.BlockSpec((256, 512), lambda i, s: (i, 1 - s[1]))
    return pl.pallas_call(
        next_kernel,
        grid_spec=pltpu.PrefetchScalarGridSpec(
            num_scalar_prefetch=1,
            grid=(2,),
            in_specs=[theirs, theirs],
            out_specs=pl.BlockSpec((256, 1024), lambda i, s: (i, 0)),
        ),
        out_shape=shape(512, 1024),
        compiler_params=params(60),
        cost_estimate=cost(2 * MIB),
        name="next_pieces",
    )(scalars, w_gate, w_up)


def arrange_kernel(place_of, s, own, other, out):
    for which, source in enumerate((own, other)):
        for sub in range(8):
            to = pl.multiple_of(place_of(s, which, sub) * 64, 64)
            out[pl.ds(to, 64), :] = source[sub * 64 : (sub + 1) * 64, :]


def arrange(scalars, own, other, place_of, name):
    columns = own.shape[1]
    spec = lambda rows: pl.BlockSpec((rows, 256), lambda i, s: (0, i))
    return pl.pallas_call(
        functools.partial(arrange_kernel, place_of),
        grid_spec=pltpu.PrefetchScalarGridSpec(
            num_scalar_prefetch=1,
            grid=(columns // 256,),
            in_specs=[spec(512)] * 2,
            out_specs=spec(1024),
        ),
        out_shape=shape(1024, columns),
        compiler_params=params(),
        cost_estimate=cost(4 * 1024 * columns),
        name=name,
    )(scalars, own, other)


def token_place(j, s, which, sub):
    c = s[2]
    bits = (None, (sub >> 2) & 1, (sub >> 1) & 1, sub & 1)
    at = []
    for core in range(2):
        order = ORDERS[j][core][::-1]
        mine = s[{"q": 3, "p": 4, "v": 5, "u": 6}[order[0]]]
        last = mine if which == 0 else 1 - mine
        at.append(
            last * WEIGHT[order[0]] + sum(bits[n] * WEIGHT[order[n]] for n in range(1, 4))
        )
    return jnp.where(c == 0, at[0], at[1])


def hidden_place(s, which, sub):
    yl = s[1] if which == 0 else 1 - s[1]
    zh, zl, yh = (sub >> 2) & 1, (sub >> 1) & 1, sub & 1
    u = 1 - yl if yh else yl
    return zh * 8 + (zl ^ zh) * 4 + yh * 2 + u


def gate_sum(spans, mine, s, refs):
    count = max(block for block, _, _ in spans) + 1
    own_now = (s[1] == s[2]) if mine else (s[1] != s[2])
    tokens = [jnp.where(own_now, refs[n][...], refs[count + n][...]) for n in range(count)]
    acc = None
    for (block, at, rows), piece in zip(spans, refs[2 * count :]):
        term = jnp.dot(tokens[block][:, at : at + rows], piece[...], preferred_element_type=F32)
        acc = term if acc is None else acc + term
    return acc


def gate_own(s, *refs):
    refs[-1][...] = gate_sum(OWN_SPANS, True, s, refs)


def gate_other(s, *refs):
    refs[-1][...] = refs[-2][...] + gate_sum(OTHER_SPANS, False, s, refs)


def gate_far(s, *refs):
    partial, hidden, delta = refs[-3:]
    total = partial[...] + gate_sum(FAR_SPANS, False, s, refs)
    gate, upper = total[:, :512], total[:, 512:]
    sigma = 1.0 / (1.0 + jnp.exp(-gate))
    grad = hidden[...].astype(F32)
    delta[:, :512] = (grad * upper * sigma * (1.0 + gate * (1.0 - sigma))).astype(BF)
    delta[:, 512:] = (grad * gate * sigma).astype(BF)


OWN_SPANS = ((0, 0, 512), (1, 0, 512), (2, 0, 256), (2, 256, 256), (3, 0, 512))
OTHER_SPANS = ((0, 0, 512), (1, 0, 512), (2, 0, 512))
FAR_SPANS = ((0, 0, 256), (0, 256, 256))
TILE = 256


def rows_of(columns, at=0):
    return pl.BlockSpec((TILE, columns), lambda i, s: (i, at))


def gate_call(kernel, scalars, tokens, blocks, pieces, more, out, name):
    picked = [(tokens[2 * side + d // 2], d % 2) for side in range(2) for d in blocks]
    return pl.pallas_call(
        kernel,
        grid_spec=pltpu.PrefetchScalarGridSpec(
            num_scalar_prefetch=1,
            grid=(1024 // TILE,),
            in_specs=[rows_of(512, at) for _, at in picked]
            + [whole(*piece.shape) for piece in pieces]
            + [rows_of(array.shape[1]) for array in more],
            out_specs=rows_of(1024),
        ),
        out_shape=shape(1024, 1024, out),
        compiler_params=params(),
        cost_estimate=cost(14 * MIB),
        name=name,
    )(scalars, *[array for array, _ in picked], *pieces, *more)


def grads_call(blocks, groups, delta, kind, name):
    count = len(blocks)
    parts = []
    for m, group in enumerate(groups):
        row = 0
        for n, start, rows in group:
            parts.append((n, start, rows, m, row))
            row += rows

    def kernel(*refs):
        columns, delta_in = refs[:count], refs[count]
        outs = refs[count + 1 : count + 1 + len(groups)]
        tokens, deltas, results, in_sems, out_sems = refs[count + 1 + len(groups) :]
        loads = [pltpu.make_async_copy(delta_in, deltas, in_sems.at[count])]
        for n in range(count):
            source = columns[n].at[:, pl.ds(blocks[n][1] * 512, 512)]
            loads.append(pltpu.make_async_copy(source, tokens.at[n], in_sems.at[n]))
        for load in loads:
            load.start()
        loads[0].wait()
        stores = []
        for n in range(count):
            loads[n + 1].wait()
            results[n] = lax.dot_general(
                tokens[n], deltas[...], (((0,), (0,)), ((), ())), preferred_element_type=F32
            ).astype(kind)
            for k, (which, start, rows, m, row) in enumerate(parts):
                if which == n:
                    source = results.at[n, pl.ds(start, rows)]
                    target = outs[m].at[pl.ds(row, rows)]
                    stores.append(pltpu.make_async_copy(source, target, out_sems.at[k]))
                    stores[-1].start()
        for store in stores:
            store.wait()

    return pl.pallas_call(
        kernel,
        in_specs=[pl.BlockSpec(memory_space=pl.ANY)] * (count + 1),
        out_specs=[pl.BlockSpec(memory_space=pl.ANY)] * len(groups),
        out_shape=[shape(sum(rows for _, _, rows in group), 1024, kind) for group in groups],
        scratch_shapes=[
            pltpu.VMEM((count, 1024, 512), BF),
            pltpu.VMEM((1024, 1024), BF),
            pltpu.VMEM((count, 512, 1024), kind),
            pltpu.SemaphoreType.DMA((count + 1,)),
            pltpu.SemaphoreType.DMA((len(parts),)),
        ],
        compiler_params=params(),
        cost_estimate=cost(10 * MIB),
        name=name,
    )(*[array for array, _ in blocks], delta)


def igrad_call(scalars, j, delta, mine, theirs):
    flat = [(array, which, d, at) for which, group in enumerate((mine, theirs))
            for d in range(2) for at, array in enumerate(group[d])]
    count = len(flat)

    def kernel(s, *refs):
        delta_in, arrays = refs[0], refs[1 : count + 1]
        own_out, *rec_outs = refs[count + 1 : count + 4]
        deltas, pieces, results, in_sems, out_sems = refs[count + 4 :]
        c = s[2]
        loads = [pltpu.make_async_copy(delta_in, deltas, in_sems.at[count])]
        for n, (array, which, d, at) in enumerate(flat):
            rows = array.shape[0]
            target = pieces.at[which, d, pl.ds(at * rows, rows)]
            loads.append(pltpu.make_async_copy(arrays[n], target, in_sems.at[n]))
        for load in loads:
            load.start()
        loads[0].wait()
        side = jnp.where(s[1] == c, 1, 0)
        stores = []
        for d in range(2):
            for n in range(count):
                if flat[n][2] == d:
                    loads[n + 1].wait()
            for turn, which, core in ((0, side, 1 - c), (1, 1 - side, c)):
                columns = slice(d * 512, (d + 1) * 512)
                piece = pieces[which, d]
                for block in range(16):
                    if block % 4 == 0:
                        acc = lax.dot_general(
                            deltas[block * 64 : block * 64 + 256],
                            piece,
                            (((1,), (1,)), ((), ())),
                            preferred_element_type=F32,
                        ).astype(BF)
                    bits = {link: (block // weight) % 2 for link, weight in WEIGHT.items()}
                    at = [sum(bits[l] << n for n, l in enumerate(order)) for order in OUT_ORDERS[j]]
                    to = pl.multiple_of(jnp.where(core == 0, at[0], at[1]) * 64, 64)
                    part = (block % 4) * 64
                    results[turn, pl.ds(to, 64), columns] = acc[part : part + 64]
                moves = [(results.at[1, :, columns], own_out.at[:, columns], 4 + d)]
                if turn == 0:
                    moves = [
                        (results.at[0, pl.ds(n * 512, 512), columns], rec_outs[n].at[:, columns], 2 * d + n)
                        for n in range(2)
                    ]
                for source, target, sem in moves:
                    stores.append(pltpu.make_async_copy(source, target, out_sems.at[sem]))
                    stores[-1].start()
        for store in stores:
            store.wait()

    return pl.pallas_call(
        kernel,
        grid_spec=pltpu.PrefetchScalarGridSpec(
            num_scalar_prefetch=1,
            grid=(),
            in_specs=[pl.BlockSpec(memory_space=pl.ANY)] * (count + 1),
            out_specs=[pl.BlockSpec(memory_space=pl.ANY)] * 3,
            scratch_shapes=[
                pltpu.VMEM((1024, 1024), BF),
                pltpu.VMEM((2, 2, 512, 1024), BF),
                pltpu.VMEM((2, 1024, 1024), BF),
                pltpu.SemaphoreType.DMA((count + 1,)),
                pltpu.SemaphoreType.DMA((6,)),
            ],
        ),
        out_shape=[shape(1024, 1024)] + [shape(512, 1024)] * 2,
        compiler_params=params(),
        cost_estimate=cost(10 * MIB),
        name="igrad",
    )(scalars, delta, *[array for array, _, _, _ in flat])


def put_kernel(s, piece, *refs):
    gate, up = refs[-2:]
    gate[...] = piece[:, :512].astype(F32)
    up[...] = piece[:, 512:].astype(F32)


def put(scalars, half, other, piece, outs):
    column = (lambda s: 1 - s[1]) if other else (lambda s: s[1])
    return pl.pallas_call(
        put_kernel,
        grid_spec=pltpu.PrefetchScalarGridSpec(
            num_scalar_prefetch=1,
            grid=(2,),
            in_specs=[pl.BlockSpec((128, 1024), lambda i, s: (i, 0))]
            + [pl.BlockSpec(memory_space=pl.ANY)] * len(outs),
            out_specs=[pl.BlockSpec((128, 512), lambda i, s: (i + 2 * half, column(s)))] * 2,
        ),
        out_shape=[shape(512, 1024, F32)] * 2,
        input_output_aliases={2 + n: n for n in range(len(outs))},
        compiler_params=params(),
        cost_estimate=cost(3 * MIB),
        name="put",
    )(scalars, piece, *outs)


def shards(inputs, hidden_grad, w_gate, w_up):
    node, local = lax.axis_index("node"), lax.axis_index("local")
    x, yl = node // 2, node % 2
    zh, zl, yh, c = local // 8, (local // 4) % 2, (local // 2) % 2, local % 2
    bit = {"q": zh, "p": (zl + zh) % 2, "v": yh, "u": (yl + yh) % 2}
    scalars = jnp.stack([x, yl, c] + [bit[link] for link in "qpvu"]).astype(jnp.int32)
    def stages_of(orders):
        return [
            [(both_cores(a, b), jnp.where(c == 0, bit[a], bit[b])) for a, b in zip(*pair)]
            for pair in orders
        ]

    stages = stages_of(ORDERS)

    keep, give, own = first_pieces(scalars, inputs, w_gate, w_up)
    own_down, own_up = send(own, XUP), send(own, XDOWN)
    other = send(next_pieces(scalars, after(w_gate, own), w_up), YLO)
    rows = join(keep, send(give, CORE), c)
    chains = [rows[:, :1024], rows[:, 1024:]]
    step = lambda n: [join(v, send(v, st[n][0]), st[n][1]) for v, st in zip(chains, stages)]
    chains = step(0)
    chains = step(1)
    chains = [after(v, own_down, own_up, other) for v in chains]
    chains = step(2)
    far_a = send(after(own_down[:256], own_up), XUP)
    far_b = send(after(own_up[256:], own_down), XDOWN)
    chains = [after(v, far_a, far_b) for v in chains]
    lasts = [send(v, st[3][0]) for v, st in zip(chains, stages)]
    h_own, h_oth = hidden_pieces(scalars, after(hidden_grad, own_down, own_up))
    h_other = send(after(h_oth, far_a, far_b), YLO)
    other = after(other, far_a, far_b)
    other_down, other_up = send(other, XUP), send(other, XDOWN)
    own_tokens = [
        arrange(scalars, v, last, functools.partial(token_place, j), "arrange")
        for j, (v, last) in enumerate(zip(chains, lasts))
    ]
    rec_tokens = [send(after(block, other_down, other_up), CORE) for block in own_tokens]
    tokens = own_tokens + rec_tokens
    other_far_a = send(after(other_down[:256], other_up), XUP)
    other_far_b = send(after(other_up[256:], other_down), XDOWN)
    partial = gate_call(
        gate_own, scalars, tokens, (0, 1, 2, 3), [own, own_up, far_a, far_b, own_down], [], F32,
        "gate_own",
    )
    partial = gate_call(
        gate_other, scalars, tokens, (0, 1, 3),
        [other, other_up, other_down], [partial], F32, "gate_other",
    )
    hidden = arrange(scalars, after(h_own, partial), h_other, hidden_place, "arrange_hidden")
    delta = gate_call(
        gate_far, scalars, tokens, (2,), [other_far_a, other_far_b], [partial, hidden], BF, "gate_far",
    )
    own_pieces = [[own], [own_up], [far_a, far_b], [own_down]]
    other_pieces = [[other], [other_up], [other_far_a, other_far_b], [other_down]]

    block = lambda side, d: (tokens[2 * side + d // 2], d % 2)
    stages = stages_of(OUT_ORDERS)

    def igrad(j, order):
        return igrad_call(
            scalars, j, order, own_pieces[2 * j : 2 * j + 2], other_pieces[2 * j : 2 * j + 2]
        )

    def core_halve(own_i, recs, stage, *deps):
        to, at = stage
        sums = [
            (own_i[n * 512 : n * 512 + 512].astype(F32) + send(rec, CORE).astype(F32)).astype(BF)
            for n, rec in enumerate(recs)
        ]
        other = send(after(jnp.where(at == 0, sums[1], sums[0]), *deps), to)
        kept = jnp.where(at == 0, sums[0], sums[1])
        return (kept.astype(F32) + other.astype(F32)).astype(BF)

    def halve(value, stage, *deps):
        to, at = stage
        halves = value.reshape(2, -1, 1024)
        other = send(after(pick(halves, 1 - at), *deps), to)
        return (pick(halves, at).astype(F32) + other.astype(F32)).astype(BF)

    full = lambda n: [(n, 0, 512)]
    plus, minus = grads_call(
        [block(0, 2), block(1, 2), block(1, 1), block(0, 3)],
        [full(0) + full(2), full(1) + full(3)], delta, BF, "away_grads",
    )
    rest_down, rest_up = send(plus, XUP), send(minus, XDOWN)
    own_0, *rec_0 = igrad(0, after(delta, plus))
    own_1, *rec_1 = igrad(1, after(delta, own_0))
    up_own, down_rec = grads_call(
        [block(0, 1), block(1, 3)], [full(0), full(1)], after(delta, own_1), F32, "pass_grads"
    )
    home_own, home_rec = grads_call(
        [block(0, 0), block(1, 0)], [full(0), full(1)], after(delta, up_own), F32, "home_grads"
    )
    sum_0 = core_halve(own_0, rec_0, stages[0][3], rest_down, rest_up)
    sum_1 = core_halve(own_1, rec_1, stages[1][3], rest_down, rest_up)
    sum_0 = halve(sum_0, stages[0][2])
    sum_1 = halve(sum_1, stages[1][2])
    sum_0 = halve(sum_0, stages[0][1])
    sum_1 = halve(sum_1, stages[1][1])
    add = lambda a, b: (a + b.astype(F32)).astype(BF)
    passed = [
        (add(up_own[at : at + 256], rest_down[at : at + 256]), add(down_rec[at : at + 256], rest_up[at : at + 256]))
        for at in (0, 256)
    ]
    ends = [(send(passed[0][0], XUP), send(passed[0][1], XDOWN))]
    up, down = lax.optimization_barrier((*passed[1], *ends[0]))[:2]
    ends.append((send(up, XUP), send(down, XDOWN)))
    near_down, near_up = after(rest_down, *passed[1])[512:], after(rest_up, *passed[1])[512:]
    sum_0 = halve(sum_0, stages[0][0])
    sum_1 = halve(sum_1, stages[1][0])
    sums = jnp.concatenate([v.reshape(2, 32, 2, 512) for v in (sum_0, sum_1)], 2)
    kept, other_sums = pick(sums, c), send(pick(sums, 1 - c), CORE)
    halves = jnp.where(c == 0, jnp.stack([kept, other_sums], 2), jnp.stack([other_sums, kept], 2))
    input_grad = jnp.take(halves.reshape(32, 4, 1024), (jnp.arange(4) - x) % 4, axis=1)

    own_sum = home_own + near_up.astype(F32)
    rec_sum = home_rec + near_down.astype(F32)
    same = yl == c
    given, kept = lax.optimization_barrier(
        (jnp.where(same, rec_sum, own_sum), jnp.where(same, own_sum, rec_sum))
    )
    outs, others, last = (), [], ()
    for half, (end_down, end_up) in enumerate(ends):
        at = slice(half * 256, half * 256 + 256)
        end_down, end_up = after(end_down, *last), after(end_up, *last)
        last = (add(given[at], jnp.where(same, end_up, end_down)),)
        others.append(send(last[0], YLO))
        end = after(jnp.where(same, end_down, end_up), *last)
        outs = put(scalars, half, False, kept[at] + end.astype(F32), outs)
    for half, other in enumerate(others):
        outs = put(scalars, half, True, other, outs)
    return input_grad.reshape(32, 4096), *outs


def solution(mesh):
    in_specs = (
        P(("node", "local"), None),
        P("node", "local"),
        P("node", "local"),
        P("node", "local"),
    )
    out_specs = (P(("node", "local"), None), P("node", "local"), P("node", "local"))
    return jax.shard_map(shards, mesh=mesh, in_specs=in_specs, out_specs=out_specs, check_vma=False)
```

```python
import functools

import jax
import jax.numpy as jnp
from jax import lax
from jax.experimental import pallas as pl
from jax.experimental.pallas import tpu as pltpu
from jax.sharding import PartitionSpec as P

AXES = ("node", "local")
BF, F32 = jnp.bfloat16, jnp.float32
MIB = 1 << 20


def place(i):
    n, l = divmod(i, 16)
    return (n // 2, n % 2, l // 4, (l // 2) % 2, l % 2)


def index(x, yl, z, yh, c):
    return (x * 2 + yl) * 16 + z * 4 + yh * 2 + c


def pairs(move):
    return [(i, index(*move(*place(i)))) for i in range(128)]


LINKS = {
    "u": lambda x, yl, z, yh, c: (x, 1 - yl, z, yh, c),
    "v": lambda x, yl, z, yh, c: (x, 1 - yl, z, 1 - yh, c),
    "p": lambda x, yl, z, yh, c: (x, yl, z ^ 1, yh, c),
    "q": lambda x, yl, z, yh, c: (x, yl, 3 - z, yh, c),
}
XUP = pairs(lambda x, yl, z, yh, c: ((x + 1) % 4, yl, z, yh, c))
XDOWN = pairs(lambda x, yl, z, yh, c: ((x + 3) % 4, yl, z, yh, c))
YLO = pairs(LINKS["u"])
CORE = pairs(lambda x, yl, z, yh, c: (x, yl, z, yh, 1 - c))
ORDERS = (("vupq", "qvup"), ("puqv", "pqvu"))
OUT_ORDERS = (("qpvu", "uqpv"), ("uvqp", "upvq"))
WEIGHT = {"q": 8, "p": 4, "v": 2, "u": 1}


def both_cores(link0, link1):
    return pairs(lambda *at: LINKS[link1 if at[4] else link0](*at))


def send(value, to):
    return lax.ppermute(value, AXES, to)


def after(value, *others):
    return lax.optimization_barrier((value, *others))[0]


def pick(value, at):
    return lax.dynamic_index_in_dim(value, at, 0, keepdims=False)


def join(own, other, bit):
    where = lax.broadcasted_iota(jnp.int32, (2,) + own.shape, 0) == bit
    both = jnp.where(where, own[None], other[None])
    return both.reshape((2 * own.shape[0],) + own.shape[1:])


def cost(bytes_):
    return pl.CostEstimate(flops=1, bytes_accessed=bytes_ // 64, transcendentals=0)


def params(mib=24):
    return pltpu.CompilerParams(vmem_limit_bytes=mib * MIB)


def shape(rows, columns, kind=BF):
    return jax.ShapeDtypeStruct((rows, columns), kind)


def whole(rows, columns):
    return pl.BlockSpec((rows, columns), lambda *_: (0, 0))


def first_kernel(s, x_ref, g_ref, u_ref, keep, give, own):
    x, c = s[0], s[2]
    own[:, :512] = g_ref[...]
    own[:, 512:] = u_ref[...]

    @pl.when(pl.program_id(0) == 0)
    def _():
        for d in range(4):
            base = lax.rem(x + d, 4) * 1024
            for out, half in ((keep, c), (give, 1 - c)):
                out[:, d * 512 : (d + 1) * 512] = x_ref[
                    :, pl.ds(pl.multiple_of(base + half * 512, 512), 512)
                ]


def first_pieces(scalars, inputs, w_gate, w_up):
    rows = lambda columns: pl.BlockSpec((256, columns), lambda i, s: (i, 0))
    mine = pl.BlockSpec((256, 512), lambda i, s: (i, s[1]))
    return pl.pallas_call(
        first_kernel,
        grid_spec=pltpu.PrefetchScalarGridSpec(
            num_scalar_prefetch=1,
            grid=(2,),
            in_specs=[whole(32, 4096), mine, mine],
            out_specs=[whole(32, 2048)] * 2 + [rows(1024)],
        ),
        out_shape=[shape(32, 2048)] * 2 + [shape(512, 1024)],
        compiler_params=params(60),
        cost_estimate=cost(4 * MIB),
        name="first_pieces",
    )(scalars, inputs, w_gate, w_up)


def next_kernel(s, g_ref, u_ref, oth):
    oth[:, :512] = g_ref[...]
    oth[:, 512:] = u_ref[...]


def hidden_kernel(s, own_ref, oth_ref, own, oth):
    own[...] = own_ref[...]
    oth[...] = oth_ref[...]


def hidden_pieces(scalars, hidden_grad):
    mine = pl.BlockSpec((256, 512), lambda i, s: (i, s[1]))
    theirs = pl.BlockSpec((256, 512), lambda i, s: (i, 1 - s[1]))
    return pl.pallas_call(
        hidden_kernel,
        grid_spec=pltpu.PrefetchScalarGridSpec(
            num_scalar_prefetch=1,
            grid=(2,),
            in_specs=[mine, theirs],
            out_specs=[pl.BlockSpec((256, 512), lambda i, s: (i, 0))] * 2,
        ),
        out_shape=[shape(512, 512)] * 2,
        compiler_params=params(),
        cost_estimate=cost(2 * MIB),
        name="hidden_pieces",
    )(scalars, hidden_grad, hidden_grad)


def next_pieces(scalars, w_gate, w_up):
    theirs = pl.BlockSpec((256, 512), lambda i, s: (i, 1 - s[1]))
    return pl.pallas_call(
        next_kernel,
        grid_spec=pltpu.PrefetchScalarGridSpec(
            num_scalar_prefetch=1,
            grid=(2,),
            in_specs=[theirs, theirs],
            out_specs=pl.BlockSpec((256, 1024), lambda i, s: (i, 0)),
        ),
        out_shape=shape(512, 1024),
        compiler_params=params(60),
        cost_estimate=cost(2 * MIB),
        name="next_pieces",
    )(scalars, w_gate, w_up)


def arrange_kernel(place_of, s, own, other, out):
    for which, source in enumerate((own, other)):
        for sub in range(8):
            to = pl.multiple_of(place_of(s, which, sub) * 64, 64)
            out[pl.ds(to, 64), :] = source[sub * 64 : (sub + 1) * 64, :]


def arrange(scalars, own, other, place_of, name):
    columns = own.shape[1]
    spec = lambda rows: pl.BlockSpec((rows, 256), lambda i, s: (0, i))
    return pl.pallas_call(
        functools.partial(arrange_kernel, place_of),
        grid_spec=pltpu.PrefetchScalarGridSpec(
            num_scalar_prefetch=1,
            grid=(columns // 256,),
            in_specs=[spec(512)] * 2,
            out_specs=spec(1024),
        ),
        out_shape=shape(1024, columns),
        compiler_params=params(),
        cost_estimate=cost(4 * 1024 * columns),
        name=name,
    )(scalars, own, other)


def token_place(j, s, which, sub):
    c = s[2]
    bits = (None, (sub >> 2) & 1, (sub >> 1) & 1, sub & 1)
    at = []
    for core in range(2):
        order = ORDERS[j][core][::-1]
        mine = s[{"q": 3, "p": 4, "v": 5, "u": 6}[order[0]]]
        last = mine if which == 0 else 1 - mine
        at.append(
            last * WEIGHT[order[0]] + sum(bits[n] * WEIGHT[order[n]] for n in range(1, 4))
        )
    return jnp.where(c == 0, at[0], at[1])


def hidden_place(s, which, sub):
    yl = s[1] if which == 0 else 1 - s[1]
    zh, zl, yh = (sub >> 2) & 1, (sub >> 1) & 1, sub & 1
    u = 1 - yl if yh else yl
    return zh * 8 + (zl ^ zh) * 4 + yh * 2 + u


def gate_sum(spans, mine, s, refs):
    count = max(block for block, _, _ in spans) + 1
    own_now = (s[1] == s[2]) if mine else (s[1] != s[2])
    tokens = [jnp.where(own_now, refs[n][...], refs[count + n][...]) for n in range(count)]
    acc = None
    for (block, at, rows), piece in zip(spans, refs[2 * count :]):
        term = jnp.dot(tokens[block][:, at : at + rows], piece[...], preferred_element_type=F32)
        acc = term if acc is None else acc + term
    return acc


def gate_own(s, *refs):
    refs[-1][...] = gate_sum(OWN_SPANS, True, s, refs)


def gate_other(s, *refs):
    refs[-1][...] = refs[-2][...] + gate_sum(OTHER_SPANS, False, s, refs)


def gate_far(s, *refs):
    partial, hidden, delta = refs[-3:]
    total = partial[...] + gate_sum(FAR_SPANS, False, s, refs)
    gate, upper = total[:, :512], total[:, 512:]
    sigma = 1.0 / (1.0 + jnp.exp(-gate))
    grad = hidden[...].astype(F32)
    delta[:, :512] = (grad * upper * sigma * (1.0 + gate * (1.0 - sigma))).astype(BF)
    delta[:, 512:] = (grad * gate * sigma).astype(BF)


OWN_SPANS = ((0, 0, 512), (1, 0, 512), (2, 0, 256), (2, 256, 256), (3, 0, 512))
OTHER_SPANS = ((0, 0, 512), (1, 0, 512), (2, 0, 512))
FAR_SPANS = ((0, 0, 256), (0, 256, 256))
TILE = 256


def rows_of(columns, at=0):
    return pl.BlockSpec((TILE, columns), lambda i, s: (i, at))


def gate_call(kernel, scalars, tokens, blocks, pieces, more, out, name):
    picked = [(tokens[2 * side + d // 2], d % 2) for side in range(2) for d in blocks]
    return pl.pallas_call(
        kernel,
        grid_spec=pltpu.PrefetchScalarGridSpec(
            num_scalar_prefetch=1,
            grid=(1024 // TILE,),
            in_specs=[rows_of(512, at) for _, at in picked]
            + [whole(*piece.shape) for piece in pieces]
            + [rows_of(array.shape[1]) for array in more],
            out_specs=rows_of(1024),
        ),
        out_shape=shape(1024, 1024, out),
        compiler_params=params(),
        cost_estimate=cost(14 * MIB),
        name=name,
    )(scalars, *[array for array, _ in picked], *pieces, *more)


def grads_call(blocks, groups, delta, kind, name):
    count = len(blocks)
    parts = []
    for m, group in enumerate(groups):
        row = 0
        for n, start, rows in group:
            parts.append((n, start, rows, m, row))
            row += rows

    def kernel(*refs):
        columns, delta_in = refs[:count], refs[count]
        outs = refs[count + 1 : count + 1 + len(groups)]
        tokens, deltas, results, in_sems, out_sems = refs[count + 1 + len(groups) :]
        loads = [pltpu.make_async_copy(delta_in, deltas, in_sems.at[count])]
        for n in range(count):
            source = columns[n].at[:, pl.ds(blocks[n][1] * 512, 512)]
            loads.append(pltpu.make_async_copy(source, tokens.at[n], in_sems.at[n]))
        for load in loads:
            load.start()
        loads[0].wait()
        stores = []
        for n in range(count):
            loads[n + 1].wait()
            results[n] = lax.dot_general(
                tokens[n], deltas[...], (((0,), (0,)), ((), ())), preferred_element_type=F32
            ).astype(kind)
            for k, (which, start, rows, m, row) in enumerate(parts):
                if which == n:
                    source = results.at[n, pl.ds(start, rows)]
                    target = outs[m].at[pl.ds(row, rows)]
                    stores.append(pltpu.make_async_copy(source, target, out_sems.at[k]))
                    stores[-1].start()
        for store in stores:
            store.wait()

    return pl.pallas_call(
        kernel,
        in_specs=[pl.BlockSpec(memory_space=pl.ANY)] * (count + 1),
        out_specs=[pl.BlockSpec(memory_space=pl.ANY)] * len(groups),
        out_shape=[shape(sum(rows for _, _, rows in group), 1024, kind) for group in groups],
        scratch_shapes=[
            pltpu.VMEM((count, 1024, 512), BF),
            pltpu.VMEM((1024, 1024), BF),
            pltpu.VMEM((count, 512, 1024), kind),
            pltpu.SemaphoreType.DMA((count + 1,)),
            pltpu.SemaphoreType.DMA((len(parts),)),
        ],
        compiler_params=params(),
        cost_estimate=cost(10 * MIB),
        name=name,
    )(*[array for array, _ in blocks], delta)


def igrad_call(scalars, j, delta, mine, theirs):
    flat = [(array, which, d, at) for which, group in enumerate((mine, theirs))
            for d in range(2) for at, array in enumerate(group[d])]
    count = len(flat)

    def kernel(s, *refs):
        delta_in, arrays = refs[0], refs[1 : count + 1]
        own_out, *rec_outs = refs[count + 1 : count + 4]
        deltas, pieces, results, in_sems, out_sems = refs[count + 4 :]
        c = s[2]
        loads = [pltpu.make_async_copy(delta_in, deltas, in_sems.at[count])]
        for n, (array, which, d, at) in enumerate(flat):
            rows = array.shape[0]
            target = pieces.at[which, d, pl.ds(at * rows, rows)]
            loads.append(pltpu.make_async_copy(arrays[n], target, in_sems.at[n]))
        for load in loads:
            load.start()
        loads[0].wait()
        side = jnp.where(s[1] == c, 1, 0)
        stores = []
        for d in range(2):
            for n in range(count):
                if flat[n][2] == d:
                    loads[n + 1].wait()
            for turn, which, core in ((0, side, 1 - c), (1, 1 - side, c)):
                columns = slice(d * 512, (d + 1) * 512)
                piece = pieces[which, d]
                for block in range(16):
                    if block % 4 == 0:
                        acc = lax.dot_general(
                            deltas[block * 64 : block * 64 + 256],
                            piece,
                            (((1,), (1,)), ((), ())),
                            preferred_element_type=F32,
                        ).astype(BF)
                    bits = {link: (block // weight) % 2 for link, weight in WEIGHT.items()}
                    at = [sum(bits[l] << n for n, l in enumerate(order)) for order in OUT_ORDERS[j]]
                    to = pl.multiple_of(jnp.where(core == 0, at[0], at[1]) * 64, 64)
                    part = (block % 4) * 64
                    results[turn, pl.ds(to, 64), columns] = acc[part : part + 64]
                moves = [(results.at[1, :, columns], own_out.at[:, columns], 4 + d)]
                if turn == 0:
                    moves = [
                        (results.at[0, pl.ds(n * 512, 512), columns], rec_outs[n].at[:, columns], 2 * d + n)
                        for n in range(2)
                    ]
                for source, target, sem in moves:
                    stores.append(pltpu.make_async_copy(source, target, out_sems.at[sem]))
                    stores[-1].start()
        for store in stores:
            store.wait()

    return pl.pallas_call(
        kernel,
        grid_spec=pltpu.PrefetchScalarGridSpec(
            num_scalar_prefetch=1,
            grid=(),
            in_specs=[pl.BlockSpec(memory_space=pl.ANY)] * (count + 1),
            out_specs=[pl.BlockSpec(memory_space=pl.ANY)] * 3,
            scratch_shapes=[
                pltpu.VMEM((1024, 1024), BF),
                pltpu.VMEM((2, 2, 512, 1024), BF),
                pltpu.VMEM((2, 1024, 1024), BF),
                pltpu.SemaphoreType.DMA((count + 1,)),
                pltpu.SemaphoreType.DMA((6,)),
            ],
        ),
        out_shape=[shape(1024, 1024)] + [shape(512, 1024)] * 2,
        compiler_params=params(),
        cost_estimate=cost(10 * MIB),
        name="igrad",
    )(scalars, delta, *[array for array, _, _, _ in flat])


def put_kernel(s, piece, *refs):
    gate, up = refs[-2:]
    gate[...] = piece[:, :512].astype(F32)
    up[...] = piece[:, 512:].astype(F32)


def put(scalars, half, other, piece, outs):
    column = (lambda s: 1 - s[1]) if other else (lambda s: s[1])
    return pl.pallas_call(
        put_kernel,
        grid_spec=pltpu.PrefetchScalarGridSpec(
            num_scalar_prefetch=1,
            grid=(2,),
            in_specs=[pl.BlockSpec((128, 1024), lambda i, s: (i, 0))]
            + [pl.BlockSpec(memory_space=pl.ANY)] * len(outs),
            out_specs=[pl.BlockSpec((128, 512), lambda i, s: (i + 2 * half, column(s)))] * 2,
        ),
        out_shape=[shape(512, 1024, F32)] * 2,
        input_output_aliases={2 + n: n for n in range(len(outs))},
        compiler_params=params(),
        cost_estimate=cost(3 * MIB),
        name="put",
    )(scalars, piece, *outs)


def shards(inputs, hidden_grad, w_gate, w_up):
    node, local = lax.axis_index("node"), lax.axis_index("local")
    x, yl = node // 2, node % 2
    zh, zl, yh, c = local // 8, (local // 4) % 2, (local // 2) % 2, local % 2
    bit = {"q": zh, "p": (zl + zh) % 2, "v": yh, "u": (yl + yh) % 2}
    scalars = jnp.stack([x, yl, c] + [bit[link] for link in "qpvu"]).astype(jnp.int32)
    def stages_of(orders):
        return [
            [(both_cores(a, b), jnp.where(c == 0, bit[a], bit[b])) for a, b in zip(*pair)]
            for pair in orders
        ]

    stages = stages_of(ORDERS)

    keep, give, own = first_pieces(scalars, inputs, w_gate, w_up)
    own_down, own_up = send(own, XUP), send(own, XDOWN)
    other = send(next_pieces(scalars, after(w_gate, own), w_up), YLO)
    rows = join(keep, send(give, CORE), c)
    chains = [rows[:, :1024], rows[:, 1024:]]
    step = lambda n: [join(v, send(v, st[n][0]), st[n][1]) for v, st in zip(chains, stages)]
    chains = step(0)
    chains = step(1)
    chains = [after(v, own_down, own_up, other) for v in chains]
    chains = step(2)
    far_a = send(after(own_down[:256], own_up), XUP)
    far_b = send(after(own_up[256:], own_down), XDOWN)
    chains = [after(v, far_a, far_b) for v in chains]
    lasts = [send(v, st[3][0]) for v, st in zip(chains, stages)]
    h_own, h_oth = hidden_pieces(scalars, after(hidden_grad, own_down, own_up))
    h_other = send(after(h_oth, far_a, far_b), YLO)
    other = after(other, far_a, far_b)
    other_down, other_up = send(other, XUP), send(other, XDOWN)
    own_tokens = [
        arrange(scalars, v, last, functools.partial(token_place, j), "arrange")
        for j, (v, last) in enumerate(zip(chains, lasts))
    ]
    rec_tokens = [send(after(block, other_down, other_up), CORE) for block in own_tokens]
    tokens = own_tokens + rec_tokens
    other_far_a = send(after(other_down[:256], other_up), XUP)
    other_far_b = send(after(other_up[256:], other_down), XDOWN)
    partial = gate_call(
        gate_own, scalars, tokens, (0, 1, 2, 3), [own, own_up, far_a, far_b, own_down], [], F32,
        "gate_own",
    )
    hidden = arrange(scalars, after(h_own, partial), h_other, hidden_place, "arrange_hidden")
    partial = gate_call(
        gate_other, scalars, [after(tokens[0], hidden), *tokens[1:]], (0, 1, 3),
        [other, other_up, other_down], [partial], F32, "gate_other",
    )
    delta = gate_call(
        gate_far, scalars, tokens, (2,), [other_far_a, other_far_b], [partial, hidden], BF, "gate_far",
    )
    own_pieces = [[own], [own_up], [far_a, far_b], [own_down]]
    other_pieces = [[other], [other_up], [other_far_a, other_far_b], [other_down]]

    block = lambda side, d: (tokens[2 * side + d // 2], d % 2)
    stages = stages_of(OUT_ORDERS)

    def igrad(j, order):
        return igrad_call(
            scalars, j, order, own_pieces[2 * j : 2 * j + 2], other_pieces[2 * j : 2 * j + 2]
        )

    def core_halve(own_i, recs, stage, *deps):
        to, at = stage
        sums = [
            (own_i[n * 512 : n * 512 + 512].astype(F32) + send(rec, CORE).astype(F32)).astype(BF)
            for n, rec in enumerate(recs)
        ]
        other = send(after(jnp.where(at == 0, sums[1], sums[0]), *deps), to)
        kept = jnp.where(at == 0, sums[0], sums[1])
        return (kept.astype(F32) + other.astype(F32)).astype(BF)

    def halve(value, stage, *deps):
        to, at = stage
        halves = value.reshape(2, -1, 1024)
        other = send(after(pick(halves, 1 - at), *deps), to)
        return (pick(halves, at).astype(F32) + other.astype(F32)).astype(BF)

    full = lambda n: [(n, 0, 512)]
    plus, minus = grads_call(
        [block(0, 2), block(1, 2), block(1, 1), block(0, 3)],
        [full(0) + full(2), full(1) + full(3)], delta, BF, "away_grads",
    )
    rest_down, rest_up = send(plus, XUP), send(minus, XDOWN)
    own_0, *rec_0 = igrad(0, after(delta, plus))
    own_1, *rec_1 = igrad(1, after(delta, own_0))
    up_own, down_rec = grads_call(
        [block(0, 1), block(1, 3)], [full(0), full(1)], after(delta, own_1), F32, "pass_grads"
    )
    home_own, home_rec = grads_call(
        [block(0, 0), block(1, 0)], [full(0), full(1)], after(delta, up_own), F32, "home_grads"
    )
    sum_0 = core_halve(own_0, rec_0, stages[0][3], rest_down, rest_up)
    sum_1 = core_halve(own_1, rec_1, stages[1][3], rest_down, rest_up)
    sum_0 = halve(sum_0, stages[0][2])
    sum_1 = halve(sum_1, stages[1][2])
    sum_0 = halve(sum_0, stages[0][1])
    sum_1 = halve(sum_1, stages[1][1])
    add = lambda a, b: (a + b.astype(F32)).astype(BF)
    passed = [
        (add(up_own[at : at + 256], rest_down[at : at + 256]), add(down_rec[at : at + 256], rest_up[at : at + 256]))
        for at in (0, 256)
    ]
    ends = [(send(passed[0][0], XUP), send(passed[0][1], XDOWN))]
    up, down = lax.optimization_barrier((*passed[1], *ends[0]))[:2]
    ends.append((send(up, XUP), send(down, XDOWN)))
    near_down, near_up = after(rest_down, *passed[1])[512:], after(rest_up, *passed[1])[512:]
    sum_0 = halve(sum_0, stages[0][0])
    sum_1 = halve(sum_1, stages[1][0])
    sums = jnp.concatenate([v.reshape(2, 32, 2, 512) for v in (sum_0, sum_1)], 2)
    kept, other_sums = pick(sums, c), send(pick(sums, 1 - c), CORE)
    halves = jnp.where(c == 0, jnp.stack([kept, other_sums], 2), jnp.stack([other_sums, kept], 2))
    input_grad = jnp.take(halves.reshape(32, 4, 1024), (jnp.arange(4) - x) % 4, axis=1)

    own_sum = home_own + near_up.astype(F32)
    rec_sum = home_rec + near_down.astype(F32)
    same = yl == c
    given, kept = lax.optimization_barrier(
        (jnp.where(same, rec_sum, own_sum), jnp.where(same, own_sum, rec_sum))
    )
    outs, others, last = (), [], ()
    for half, (end_down, end_up) in enumerate(ends):
        at = slice(half * 256, half * 256 + 256)
        end_down, end_up = after(end_down, *last), after(end_up, *last)
        last = (add(given[at], jnp.where(same, end_up, end_down)),)
        others.append(send(last[0], YLO))
        end = after(jnp.where(same, end_down, end_up), *last)
        outs = put(scalars, half, False, kept[at] + end.astype(F32), outs)
    for half, other in enumerate(others):
        outs = put(scalars, half, True, other, outs)
    return input_grad.reshape(32, 4096), *outs


def solution(mesh):
    in_specs = (
        P(("node", "local"), None),
        P("node", "local"),
        P("node", "local"),
        P("node", "local"),
    )
    out_specs = (P(("node", "local"), None), P("node", "local"), P("node", "local"))
    return jax.shard_map(shards, mesh=mesh, in_specs=in_specs, out_specs=out_specs, check_vma=False)
```

```python
import functools

import jax
import jax.numpy as jnp
from jax import lax
from jax.experimental import pallas as pl
from jax.experimental.pallas import tpu as pltpu
from jax.sharding import PartitionSpec as P

AXES = ("node", "local")
BF, F32 = jnp.bfloat16, jnp.float32
MIB = 1 << 20


def place(i):
    n, l = divmod(i, 16)
    return (n // 2, n % 2, l // 4, (l // 2) % 2, l % 2)


def index(x, yl, z, yh, c):
    return (x * 2 + yl) * 16 + z * 4 + yh * 2 + c


def pairs(move):
    return [(i, index(*move(*place(i)))) for i in range(128)]


LINKS = {
    "u": lambda x, yl, z, yh, c: (x, 1 - yl, z, yh, c),
    "v": lambda x, yl, z, yh, c: (x, 1 - yl, z, 1 - yh, c),
    "p": lambda x, yl, z, yh, c: (x, yl, z ^ 1, yh, c),
    "q": lambda x, yl, z, yh, c: (x, yl, 3 - z, yh, c),
}
XUP = pairs(lambda x, yl, z, yh, c: ((x + 1) % 4, yl, z, yh, c))
XDOWN = pairs(lambda x, yl, z, yh, c: ((x + 3) % 4, yl, z, yh, c))
YLO = pairs(LINKS["u"])
CORE = pairs(lambda x, yl, z, yh, c: (x, yl, z, yh, 1 - c))
ORDERS = (("vupq", "qvup"), ("puqv", "pqvu"))
OUT_ORDERS = (("qpvu", "uqpv"), ("uvqp", "upvq"))
WEIGHT = {"q": 8, "p": 4, "v": 2, "u": 1}


def both_cores(link0, link1):
    return pairs(lambda *at: LINKS[link1 if at[4] else link0](*at))


def send(value, to):
    return lax.ppermute(value, AXES, to)


def after(value, *others):
    return lax.optimization_barrier((value, *others))[0]


def pick(value, at):
    return lax.dynamic_index_in_dim(value, at, 0, keepdims=False)


def join(own, other, bit):
    where = lax.broadcasted_iota(jnp.int32, (2,) + own.shape, 0) == bit
    both = jnp.where(where, own[None], other[None])
    return both.reshape((2 * own.shape[0],) + own.shape[1:])


def cost(bytes_):
    return pl.CostEstimate(flops=1, bytes_accessed=bytes_ // 64, transcendentals=0)


def params(mib=24):
    return pltpu.CompilerParams(vmem_limit_bytes=mib * MIB)


def shape(rows, columns, kind=BF):
    return jax.ShapeDtypeStruct((rows, columns), kind)


def whole(rows, columns):
    return pl.BlockSpec((rows, columns), lambda *_: (0, 0))


def first_kernel(s, x_ref, g_ref, u_ref, keep, give, own):
    x, c = s[0], s[2]
    own[:, :512] = g_ref[...]
    own[:, 512:] = u_ref[...]

    @pl.when(pl.program_id(0) == 0)
    def _():
        for d in range(4):
            base = lax.rem(x + d, 4) * 1024
            for out, half in ((keep, c), (give, 1 - c)):
                out[:, d * 512 : (d + 1) * 512] = x_ref[
                    :, pl.ds(pl.multiple_of(base + half * 512, 512), 512)
                ]


def first_pieces(scalars, inputs, w_gate, w_up):
    rows = lambda columns: pl.BlockSpec((256, columns), lambda i, s: (i, 0))
    mine = pl.BlockSpec((256, 512), lambda i, s: (i, s[1]))
    return pl.pallas_call(
        first_kernel,
        grid_spec=pltpu.PrefetchScalarGridSpec(
            num_scalar_prefetch=1,
            grid=(2,),
            in_specs=[whole(32, 4096), mine, mine],
            out_specs=[whole(32, 2048)] * 2 + [rows(1024)],
        ),
        out_shape=[shape(32, 2048)] * 2 + [shape(512, 1024)],
        compiler_params=params(60),
        cost_estimate=cost(4 * MIB),
        name="first_pieces",
    )(scalars, inputs, w_gate, w_up)


def next_kernel(s, g_ref, u_ref, oth):
    oth[:, :512] = g_ref[...]
    oth[:, 512:] = u_ref[...]


def hidden_kernel(s, own_ref, oth_ref, own, oth):
    own[...] = own_ref[...]
    oth[...] = oth_ref[...]


def hidden_pieces(scalars, hidden_grad):
    mine = pl.BlockSpec((256, 512), lambda i, s: (i, s[1]))
    theirs = pl.BlockSpec((256, 512), lambda i, s: (i, 1 - s[1]))
    return pl.pallas_call(
        hidden_kernel,
        grid_spec=pltpu.PrefetchScalarGridSpec(
            num_scalar_prefetch=1,
            grid=(2,),
            in_specs=[mine, theirs],
            out_specs=[pl.BlockSpec((256, 512), lambda i, s: (i, 0))] * 2,
        ),
        out_shape=[shape(512, 512)] * 2,
        compiler_params=params(),
        cost_estimate=cost(2 * MIB),
        name="hidden_pieces",
    )(scalars, hidden_grad, hidden_grad)


def next_pieces(scalars, w_gate, w_up):
    theirs = pl.BlockSpec((256, 512), lambda i, s: (i, 1 - s[1]))
    return pl.pallas_call(
        next_kernel,
        grid_spec=pltpu.PrefetchScalarGridSpec(
            num_scalar_prefetch=1,
            grid=(2,),
            in_specs=[theirs, theirs],
            out_specs=pl.BlockSpec((256, 1024), lambda i, s: (i, 0)),
        ),
        out_shape=shape(512, 1024),
        compiler_params=params(60),
        cost_estimate=cost(2 * MIB),
        name="next_pieces",
    )(scalars, w_gate, w_up)


def arrange_kernel(place_of, s, own, other, out):
    for which, source in enumerate((own, other)):
        for sub in range(8):
            to = pl.multiple_of(place_of(s, which, sub) * 64, 64)
            out[pl.ds(to, 64), :] = source[sub * 64 : (sub + 1) * 64, :]


def arrange(scalars, own, other, place_of, name):
    columns = own.shape[1]
    spec = lambda rows: pl.BlockSpec((rows, 256), lambda i, s: (0, i))
    return pl.pallas_call(
        functools.partial(arrange_kernel, place_of),
        grid_spec=pltpu.PrefetchScalarGridSpec(
            num_scalar_prefetch=1,
            grid=(columns // 256,),
            in_specs=[spec(512)] * 2,
            out_specs=spec(1024),
        ),
        out_shape=shape(1024, columns),
        compiler_params=params(),
        cost_estimate=cost(4 * 1024 * columns),
        name=name,
    )(scalars, own, other)


def token_place(j, s, which, sub):
    c = s[2]
    bits = (None, (sub >> 2) & 1, (sub >> 1) & 1, sub & 1)
    at = []
    for core in range(2):
        order = ORDERS[j][core][::-1]
        mine = s[{"q": 3, "p": 4, "v": 5, "u": 6}[order[0]]]
        last = mine if which == 0 else 1 - mine
        at.append(
            last * WEIGHT[order[0]] + sum(bits[n] * WEIGHT[order[n]] for n in range(1, 4))
        )
    return jnp.where(c == 0, at[0], at[1])


def hidden_place(s, which, sub):
    yl = s[1] if which == 0 else 1 - s[1]
    zh, zl, yh = (sub >> 2) & 1, (sub >> 1) & 1, sub & 1
    u = 1 - yl if yh else yl
    return zh * 8 + (zl ^ zh) * 4 + yh * 2 + u


def gate_sum(spans, mine, s, refs):
    count = max(block for block, _, _ in spans) + 1
    own_now = (s[1] == s[2]) if mine else (s[1] != s[2])
    tokens = [jnp.where(own_now, refs[n][...], refs[count + n][...]) for n in range(count)]
    acc = None
    for (block, at, rows), piece in zip(spans, refs[2 * count :]):
        term = jnp.dot(tokens[block][:, at : at + rows], piece[...], preferred_element_type=F32)
        acc = term if acc is None else acc + term
    return acc


def gate_own(s, *refs):
    refs[-1][...] = gate_sum(OWN_SPANS, True, s, refs)


def gate_other(s, *refs):
    refs[-1][...] = refs[-2][...] + gate_sum(OTHER_SPANS, False, s, refs)


def gate_far(s, *refs):
    partial, hidden, delta = refs[-3:]
    total = partial[...] + gate_sum(FAR_SPANS, False, s, refs)
    gate, upper = total[:, :512], total[:, 512:]
    sigma = 1.0 / (1.0 + jnp.exp(-gate))
    grad = hidden[...].astype(F32)
    delta[:, :512] = (grad * upper * sigma * (1.0 + gate * (1.0 - sigma))).astype(BF)
    delta[:, 512:] = (grad * gate * sigma).astype(BF)


OWN_SPANS = ((0, 0, 512), (1, 0, 512), (2, 0, 256), (2, 256, 256), (3, 0, 512))
OTHER_SPANS = ((0, 0, 512), (1, 0, 512), (2, 0, 512))
FAR_SPANS = ((0, 0, 256), (0, 256, 256))
TILE = 256


def rows_of(columns, at=0):
    return pl.BlockSpec((TILE, columns), lambda i, s: (i, at))


def gate_call(kernel, scalars, tokens, blocks, pieces, more, out, name):
    picked = [(tokens[2 * side + d // 2], d % 2) for side in range(2) for d in blocks]
    return pl.pallas_call(
        kernel,
        grid_spec=pltpu.PrefetchScalarGridSpec(
            num_scalar_prefetch=1,
            grid=(1024 // TILE,),
            in_specs=[rows_of(512, at) for _, at in picked]
            + [whole(*piece.shape) for piece in pieces]
            + [rows_of(array.shape[1]) for array in more],
            out_specs=rows_of(1024),
        ),
        out_shape=shape(1024, 1024, out),
        compiler_params=params(),
        cost_estimate=cost(14 * MIB),
        name=name,
    )(scalars, *[array for array, _ in picked], *pieces, *more)


def grads_call(blocks, groups, delta, kind, name):
    count = len(blocks)
    parts = []
    for m, group in enumerate(groups):
        row = 0
        for n, start, rows in group:
            parts.append((n, start, rows, m, row))
            row += rows

    def kernel(*refs):
        columns, delta_in = refs[:count], refs[count]
        outs = refs[count + 1 : count + 1 + len(groups)]
        tokens, deltas, results, in_sems, out_sems = refs[count + 1 + len(groups) :]
        loads = [pltpu.make_async_copy(delta_in, deltas, in_sems.at[count])]
        for n in range(count):
            source = columns[n].at[:, pl.ds(blocks[n][1] * 512, 512)]
            loads.append(pltpu.make_async_copy(source, tokens.at[n], in_sems.at[n]))
        for load in loads:
            load.start()
        loads[0].wait()
        stores = []
        for n in range(count):
            loads[n + 1].wait()
            results[n] = lax.dot_general(
                tokens[n], deltas[...], (((0,), (0,)), ((), ())), preferred_element_type=F32
            ).astype(kind)
            for k, (which, start, rows, m, row) in enumerate(parts):
                if which == n:
                    source = results.at[n, pl.ds(start, rows)]
                    target = outs[m].at[pl.ds(row, rows)]
                    stores.append(pltpu.make_async_copy(source, target, out_sems.at[k]))
                    stores[-1].start()
        for store in stores:
            store.wait()

    return pl.pallas_call(
        kernel,
        in_specs=[pl.BlockSpec(memory_space=pl.ANY)] * (count + 1),
        out_specs=[pl.BlockSpec(memory_space=pl.ANY)] * len(groups),
        out_shape=[shape(sum(rows for _, _, rows in group), 1024, kind) for group in groups],
        scratch_shapes=[
            pltpu.VMEM((count, 1024, 512), BF),
            pltpu.VMEM((1024, 1024), BF),
            pltpu.VMEM((count, 512, 1024), kind),
            pltpu.SemaphoreType.DMA((count + 1,)),
            pltpu.SemaphoreType.DMA((len(parts),)),
        ],
        compiler_params=params(),
        cost_estimate=cost(10 * MIB),
        name=name,
    )(*[array for array, _ in blocks], delta)


def igrad_call(scalars, j, delta, mine, theirs):
    flat = [(array, which, d, at) for which, group in enumerate((mine, theirs))
            for d in range(2) for at, array in enumerate(group[d])]
    count = len(flat)

    def kernel(s, *refs):
        delta_in, arrays = refs[0], refs[1 : count + 1]
        own_out, *rec_outs = refs[count + 1 : count + 4]
        deltas, pieces, results, in_sems, out_sems = refs[count + 4 :]
        c = s[2]
        loads = [pltpu.make_async_copy(delta_in, deltas, in_sems.at[count])]
        for n, (array, which, d, at) in enumerate(flat):
            rows = array.shape[0]
            target = pieces.at[which, d, pl.ds(at * rows, rows)]
            loads.append(pltpu.make_async_copy(arrays[n], target, in_sems.at[n]))
        for load in loads:
            load.start()
        loads[0].wait()
        side = jnp.where(s[1] == c, 1, 0)
        stores = []
        for d in range(2):
            for n in range(count):
                if flat[n][2] == d:
                    loads[n + 1].wait()
            for turn, which, core in ((0, side, 1 - c), (1, 1 - side, c)):
                columns = slice(d * 512, (d + 1) * 512)
                piece = pieces[which, d]
                for block in range(16):
                    if block % 4 == 0:
                        acc = lax.dot_general(
                            deltas[block * 64 : block * 64 + 256],
                            piece,
                            (((1,), (1,)), ((), ())),
                            preferred_element_type=F32,
                        ).astype(BF)
                    bits = {link: (block // weight) % 2 for link, weight in WEIGHT.items()}
                    at = [sum(bits[l] << n for n, l in enumerate(order)) for order in OUT_ORDERS[j]]
                    to = pl.multiple_of(jnp.where(core == 0, at[0], at[1]) * 64, 64)
                    part = (block % 4) * 64
                    results[turn, pl.ds(to, 64), columns] = acc[part : part + 64]
                moves = [(results.at[1, :, columns], own_out.at[:, columns], 4 + d)]
                if turn == 0:
                    moves = [
                        (results.at[0, pl.ds(n * 512, 512), columns], rec_outs[n].at[:, columns], 2 * d + n)
                        for n in range(2)
                    ]
                for source, target, sem in moves:
                    stores.append(pltpu.make_async_copy(source, target, out_sems.at[sem]))
                    stores[-1].start()
        for store in stores:
            store.wait()

    return pl.pallas_call(
        kernel,
        grid_spec=pltpu.PrefetchScalarGridSpec(
            num_scalar_prefetch=1,
            grid=(),
            in_specs=[pl.BlockSpec(memory_space=pl.ANY)] * (count + 1),
            out_specs=[pl.BlockSpec(memory_space=pl.ANY)] * 3,
            scratch_shapes=[
                pltpu.VMEM((1024, 1024), BF),
                pltpu.VMEM((2, 2, 512, 1024), BF),
                pltpu.VMEM((2, 1024, 1024), BF),
                pltpu.SemaphoreType.DMA((count + 1,)),
                pltpu.SemaphoreType.DMA((6,)),
            ],
        ),
        out_shape=[shape(1024, 1024)] + [shape(512, 1024)] * 2,
        compiler_params=params(),
        cost_estimate=cost(10 * MIB),
        name="igrad",
    )(scalars, delta, *[array for array, _, _, _ in flat])


def put_kernel(s, piece, *refs):
    gate, up = refs[-2:]
    gate[...] = piece[:, :512].astype(F32)
    up[...] = piece[:, 512:].astype(F32)


def put(scalars, half, other, piece, outs):
    column = (lambda s: 1 - s[1]) if other else (lambda s: s[1])
    return pl.pallas_call(
        put_kernel,
        grid_spec=pltpu.PrefetchScalarGridSpec(
            num_scalar_prefetch=1,
            grid=(2,),
            in_specs=[pl.BlockSpec((128, 1024), lambda i, s: (i, 0))]
            + [pl.BlockSpec(memory_space=pl.ANY)] * len(outs),
            out_specs=[pl.BlockSpec((128, 512), lambda i, s: (i + 2 * half, column(s)))] * 2,
        ),
        out_shape=[shape(512, 1024, F32)] * 2,
        input_output_aliases={2 + n: n for n in range(len(outs))},
        compiler_params=params(),
        cost_estimate=cost(3 * MIB),
        name="put",
    )(scalars, piece, *outs)


def shards(inputs, hidden_grad, w_gate, w_up):
    node, local = lax.axis_index("node"), lax.axis_index("local")
    x, yl = node // 2, node % 2
    zh, zl, yh, c = local // 8, (local // 4) % 2, (local // 2) % 2, local % 2
    bit = {"q": zh, "p": (zl + zh) % 2, "v": yh, "u": (yl + yh) % 2}
    scalars = jnp.stack([x, yl, c] + [bit[link] for link in "qpvu"]).astype(jnp.int32)
    def stages_of(orders):
        return [
            [(both_cores(a, b), jnp.where(c == 0, bit[a], bit[b])) for a, b in zip(*pair)]
            for pair in orders
        ]

    stages = stages_of(ORDERS)

    keep, give, own = first_pieces(scalars, inputs, w_gate, w_up)
    own_down, own_up = send(own, XUP), send(own, XDOWN)
    other = send(next_pieces(scalars, after(w_gate, own), w_up), YLO)
    rows = join(keep, send(give, CORE), c)
    chains = [rows[:, :1024], rows[:, 1024:]]
    step = lambda n: [join(v, send(v, st[n][0]), st[n][1]) for v, st in zip(chains, stages)]
    chains = step(0)
    chains = step(1)
    chains = [after(v, own_down, own_up, other) for v in chains]
    chains = step(2)
    far_a = send(after(own_down[:256], own_up), XUP)
    far_b = send(after(own_up[256:], own_down), XDOWN)
    chains = [after(v, far_a, far_b) for v in chains]
    lasts = [send(v, st[3][0]) for v, st in zip(chains, stages)]
    h_own, h_oth = hidden_pieces(scalars, after(hidden_grad, own_down, own_up))
    h_other = send(after(h_oth, far_a, far_b), YLO)
    other = after(other, far_a, far_b)
    other_down, other_up = send(other, XUP), send(other, XDOWN)
    own_tokens = [
        arrange(scalars, v, last, functools.partial(token_place, j), "arrange")
        for j, (v, last) in enumerate(zip(chains, lasts))
    ]
    rec_tokens = [send(after(block, other_down, other_up), CORE) for block in own_tokens]
    tokens = own_tokens + rec_tokens
    other_far_a = send(after(other_down[:256], other_up), XUP)
    other_far_b = send(after(other_up[256:], other_down), XDOWN)
    partial = gate_call(
        gate_own, scalars, tokens, (0, 1, 2, 3), [own, own_up, far_a, far_b, own_down], [], F32,
        "gate_own",
    )
    hidden = arrange(scalars, after(h_own, partial), h_other, hidden_place, "arrange_hidden")
    partial = gate_call(
        gate_other, scalars, [after(tokens[0], hidden), *tokens[1:]], (0, 1, 3),
        [other, other_up, other_down], [partial], F32, "gate_other",
    )
    delta = gate_call(
        gate_far, scalars, tokens, (2,), [other_far_a, other_far_b], [partial, hidden], BF, "gate_far",
    )
    own_pieces = [[own], [own_up], [far_a, far_b], [own_down]]
    other_pieces = [[other], [other_up], [other_far_a, other_far_b], [other_down]]

    block = lambda side, d: (tokens[2 * side + d // 2], d % 2)
    stages = stages_of(OUT_ORDERS)

    def igrad(j, order):
        return igrad_call(
            scalars, j, order, own_pieces[2 * j : 2 * j + 2], other_pieces[2 * j : 2 * j + 2]
        )

    def core_halve(own_i, recs, stage, *deps):
        to, at = stage
        sums = [
            (own_i[n * 512 : n * 512 + 512].astype(F32) + send(rec, CORE).astype(F32)).astype(BF)
            for n, rec in enumerate(recs)
        ]
        other = send(after(jnp.where(at == 0, sums[1], sums[0]), *deps), to)
        kept = jnp.where(at == 0, sums[0], sums[1])
        return (kept.astype(F32) + other.astype(F32)).astype(BF)

    def halve(value, stage, *deps):
        to, at = stage
        halves = value.reshape(2, -1, 1024)
        other = send(after(pick(halves, 1 - at), *deps), to)
        return (pick(halves, at).astype(F32) + other.astype(F32)).astype(BF)

    full = lambda n: [(n, 0, 512)]
    plus, minus = grads_call(
        [block(0, 2), block(1, 2), block(1, 1), block(0, 3)],
        [full(0) + full(2), full(1) + full(3)], delta, BF, "away_grads",
    )
    rest_down, rest_up = send(plus, XUP), send(minus, XDOWN)
    own_0, *rec_0 = igrad(0, after(delta, plus))
    own_1, *rec_1 = igrad(1, after(delta, own_0))
    up_own, down_rec = grads_call(
        [block(0, 1), block(1, 3)], [full(0), full(1)], after(delta, own_1), F32, "pass_grads"
    )
    home_own, home_rec = grads_call(
        [block(0, 0), block(1, 0)], [full(0), full(1)], after(delta, up_own), F32, "home_grads"
    )
    sum_0 = core_halve(own_0, rec_0, stages[0][3], rest_down, rest_up)
    sum_1 = core_halve(own_1, rec_1, stages[1][3], rest_down, rest_up)
    sum_0 = halve(sum_0, stages[0][2])
    sum_1 = halve(sum_1, stages[1][2])
    sum_0 = halve(sum_0, stages[0][1])
    sum_1 = halve(sum_1, stages[1][1])
    add = lambda a, b: (a + b.astype(F32)).astype(BF)
    passed = [
        (add(up_own[at : at + 256], rest_down[at : at + 256]), add(down_rec[at : at + 256], rest_up[at : at + 256]))
        for at in (0, 256)
    ]
    ends = [(send(passed[0][0], XUP), send(passed[0][1], XDOWN))]
    up, down = lax.optimization_barrier((*passed[1], *ends[0]))[:2]
    ends.append((send(up, XUP), send(down, XDOWN)))
    near_down, near_up = after(rest_down, *passed[1])[512:], after(rest_up, *passed[1])[512:]
    own_sum = home_own + near_up.astype(F32)
    rec_sum = home_rec + near_down.astype(F32)
    same = yl == c
    given, kept = lax.optimization_barrier(
        (jnp.where(same, rec_sum, own_sum), jnp.where(same, own_sum, rec_sum))
    )
    outs, others, last = (), [], ()
    for half, (end_down, end_up) in enumerate(ends):
        at = slice(half * 256, half * 256 + 256)
        end_down, end_up = after(end_down, *last), after(end_up, *last)
        last = (add(given[at], jnp.where(same, end_up, end_down)),)
        others.append(send(last[0], YLO))
        end = after(jnp.where(same, end_down, end_up), *last)
        outs = put(scalars, half, False, kept[at] + end.astype(F32), outs)
    sum_0 = halve(sum_0, stages[0][0])
    sum_1 = halve(sum_1, stages[1][0], outs[0])
    sums = jnp.concatenate([v.reshape(2, 32, 2, 512) for v in (sum_0, sum_1)], 2)
    kept, other_sums = pick(sums, c), send(pick(sums, 1 - c), CORE)
    halves = jnp.where(c == 0, jnp.stack([kept, other_sums], 2), jnp.stack([other_sums, kept], 2))
    input_grad = jnp.take(halves.reshape(32, 4, 1024), (jnp.arange(4) - x) % 4, axis=1)

    for half, other in enumerate(others):
        outs = put(scalars, half, True, other, outs)
    return input_grad.reshape(32, 4096), *outs


def solution(mesh):
    in_specs = (
        P(("node", "local"), None),
        P("node", "local"),
        P("node", "local"),
        P("node", "local"),
    )
    out_specs = (P(("node", "local"), None), P("node", "local"), P("node", "local"))
    return jax.shard_map(shards, mesh=mesh, in_specs=in_specs, out_specs=out_specs, check_vma=False)
```
